32 devices in a mesh: age: 8 (over y, x, core), box: 4 (over z).
Axes of the slice: x: 2, y: 2, z: 4, core: 2. Of those that a mesh axis runs over, the one named last changes fastest.
Arguments:
- position: float32 [3, 131072], P(None, ('age', 'box')), may hold values from -6 to 6
- strength: float32 [3, 131072], P(None, ('age', 'box')), may hold values from -6 to 6
- node_box: int32 [131072], P(('age', 'box')), may hold values from 0 to 1023, as said below
- box_order: int32 [1024], P(('age', 'box')), may hold values from 0 to 1023, as said below
- box_center: float32 [3, 1024], P(None, ('age', 'box')), may hold values from -6 to 6
- near_list: int32 [1024, 4], P(('age', 'box')), may hold values from -1 to 1023, as said below
- m2l_source: int32 [1024, 32], P(('age', 'box')), may hold values from 0 to 1023
- m2l_type: int32 [1024, 32], P(('age', 'box')), may hold values from 0 to 15
- basis_dir: float32 [3, 256], replicated, may hold values from -3.5 to 3.5
- basis_freq: float32 [3, 256], replicated, may hold values from -6 to 6
- basis_phase: float32 [256], replicated, may hold values from -3.140625 to 3.140625
- translation: bfloat16 [16, 256, 256], replicated, may hold values from -0.0012207031 to 0.0012207031
Outputs:
- velocity: float32 [3, 131072], P(None, ('age', 'box'))
The draws below stay inside these ranges and needn't reach their ends.
Inputs may be any that keep to these rules, and one draw needn't show every extreme that they name: box_order is a permutation of the box ids. `node_box`: every entry is a box id. Of the 4096 nodes of one device (aligned blocks of 4096 entries), at most 256 lie in the boxes held by any one device, that is the boxes box_order[g * 32] to box_order[g * 32 + 31]; in every draw some device holds the boxes of exactly 256 nodes of every device. Over all nodes, at most 256 lie in any one box, and in every draw some box holds exactly 256. `near_list`: row p lists box_order[p] first, then distinct other boxes held by the same device as position p, then -1 padding. `m2l_source`: entries are box ids; repeats may occur.
All inputs are finite; a program needn't handle non-finite values.
Results may differ from the reference program's by a relative error of at most 0.0025.
Values may be sent and summed in bfloat16 or wider, within the bound.
A program may use at most 64 MiB of HBM per device.

```python
import jax
import jax.numpy as jnp
from jax import lax

NODE_DEV = 4096
BOX_DEV = 32
COEF = 256
TYPES = 16
LIST = 32
NEAR = 4
GROUPS = 32
CAP = 256
NODES = 131072
BOXES = 1024
N_AGE = 8
N_BOX = 4


def owner_order(key):
    return jax.random.permutation(jax.random.fold_in(key, 11), BOXES).astype(jnp.int32)


def draw_box_order(key, part):
    return owner_order(key)


def draw_node_box(key, part):
    order_table = owner_order(key)
    hottest = jax.random.randint(jax.random.fold_in(key, 12), (), 0, GROUPS).astype(jnp.int32)
    label_count = (GROUPS - 1) * CAP
    group_ids = jnp.arange(GROUPS, dtype=jnp.int32)

    def one_source(source_key):
        picks = jax.random.permutation(jax.random.fold_in(source_key, 1), label_count)[:NODE_DEV - CAP]
        target = (picks // CAP).astype(jnp.int32)
        target = target + (target >= hottest).astype(jnp.int32)
        target = jnp.concatenate([jnp.full((CAP,), 1, jnp.int32) * hottest, target])
        target = jax.random.permutation(jax.random.fold_in(source_key, 2), target)
        target_hits = (target[:, None] == group_ids[None, :]).astype(jnp.int32)
        rank_in = jnp.sum(jnp.cumsum(target_hits, axis=0) * target_hits, axis=1) - 1
        rotation = jax.random.randint(jax.random.fold_in(source_key, 3), (GROUPS,), 0, BOX_DEV).astype(jnp.int32)
        within = ((rank_in + rotation[target]) % BOX_DEV).astype(jnp.int32)
        return order_table[target * BOX_DEV + within]
    source_keys = jax.random.split(jax.random.fold_in(key, 13), GROUPS)
    return jax.vmap(one_source)(source_keys).reshape(-1).astype(jnp.int32)


def draw_near_list(key, part):
    order_table = owner_order(key)
    row_ids = jnp.arange(BOXES, dtype=jnp.int32)
    local_idx = row_ids % BOX_DEV
    base_row = row_ids - local_idx

    def one_row(row_key):
        return jax.random.permutation(row_key, BOX_DEV - 1)[:NEAR - 1].astype(jnp.int32)
    picks = jax.vmap(one_row)(jax.random.split(jax.random.fold_in(key, 14), BOXES))
    others = base_row[:, None] + (local_idx[:, None] + 1 + picks) % BOX_DEV
    kept = jax.random.randint(jax.random.fold_in(key, 15), (BOXES,), 1, NEAR + 1).astype(jnp.int32)
    kept = jnp.where(local_idx == 0, NEAR, jnp.where(local_idx == 1, 1, kept))
    entries = jnp.concatenate([row_ids[:, None], others], axis=1)
    keep_flag = jnp.arange(NEAR, dtype=jnp.int32)[None, :] < kept[:, None]
    return jnp.where(keep_flag, order_table[entries], -1).astype(jnp.int32)


def place_ends(values, rng, low, largest):
    longest = values.shape.index(max(values.shape))
    spots = []
    for shift in (0, 1):
        where = [jax.random.randint(jax.random.fold_in(rng, axis), (), 0, length) for axis, length in enumerate(values.shape)]
        where[longest] = (where[longest] + shift) % values.shape[longest]
        spots.append(tuple(where))
    return values.at[spots[0]].set(low).at[spots[1]].set(largest)


def block_scale(stream_key, shape, cuts, smallest, top_value):
    def one(dim, parts):
        draws = jax.random.uniform(jax.random.fold_in(jax.random.fold_in(stream_key, 6), dim), (parts,), jnp.float32, smallest / len(cuts), top_value / len(cuts))
        return jnp.repeat(jnp.exp(draws), shape[dim] // parts).reshape((-1,) + (1,) * (len(shape) - dim - 1))

    loudness = one(*cuts[0])
    for cut in cuts[1:]:
        loudness = loudness * one(*cut)
    return loudness


def bell_draw(rng, shape, scale, reach, cuts=(), kind=jnp.bfloat16):
    drawn = scale * jax.random.normal(rng, shape, jnp.float32)
    if cuts:
        drawn = drawn * block_scale(rng, shape, cuts, -0.22, 0.18)
    return jnp.clip(drawn, -reach, reach).astype(kind)


def setup_inputs(seed: int = 0) -> dict:
    key_list = jax.random.split(jax.random.key(seed), 13)
    return {
        "position": bell_draw(key_list[0], (3, NODES), 1.0, 6.0, ((1, 32),), jnp.float32),
        "strength": bell_draw(key_list[1], (3, NODES), 1.0, 6.0, ((1, 32),), jnp.float32),
        "node_box": draw_node_box(jax.random.fold_in(key_list[12], 71), 0),
        "box_order": draw_box_order(jax.random.fold_in(key_list[12], 71), 0),
        "box_center": bell_draw(key_list[4], (3, BOXES), 1.0, 6.0, ((1, 32),), jnp.float32),
        "near_list": draw_near_list(jax.random.fold_in(key_list[12], 71), 0),
        "m2l_source": place_ends(jax.random.randint(key_list[6], (BOXES, LIST), 0, BOXES), jax.random.fold_in(key_list[6], 1), 0, BOXES - 1).astype(jnp.int32),
        "m2l_type": place_ends(jax.random.randint(key_list[7], (BOXES, LIST), 0, TYPES), jax.random.fold_in(key_list[7], 1), 0, TYPES - 1).astype(jnp.int32),
        "basis_dir": bell_draw(key_list[8], (3, COEF), 3 ** -0.5, 3.5, (), jnp.float32),
        "basis_freq": bell_draw(key_list[9], (3, COEF), 1.5, 6.0, (), jnp.float32),
        "basis_phase": jnp.clip(jax.random.uniform(key_list[10], (COEF,), jnp.float32, -3.140625, 3.140625), -3.140625, 3.140625),
        "translation": bell_draw(key_list[11], (TYPES, COEF, COEF), (20 * COEF * LIST * NODE_DEV // BOX_DEV) ** -0.5, 0.0012207031),
    }


core_square = 0.01
inv_four_pi = 0.07957747154594767

def expansion(offsets, charges, basis_dir, basis_freq, basis_phase):
    phase_arg = basis_freq[0][:, None] * offsets[0][None, :] + basis_freq[1][:, None] * offsets[1][None, :] + basis_freq[2][:, None] * offsets[2][None, :] + basis_phase[:, None]
    wave_vals = jnp.cos(phase_arg)
    weight = basis_dir[0][:, None] * charges[0][None, :] + basis_dir[1][:, None] * charges[1][None, :] + basis_dir[2][:, None] * charges[2][None, :]
    return (wave_vals, weight)

def near_field(target_pos, source_pos, source_str, pair_mask):
    delta_x = target_pos[0][:, None] - source_pos[0][None, :]
    delta_y = target_pos[1][:, None] - source_pos[1][None, :]
    delta_z = target_pos[2][:, None] - source_pos[2][None, :]
    distance = delta_x * delta_x + delta_y * delta_y + delta_z * delta_z + core_square
    factor = pair_mask * inv_four_pi / (distance * jnp.sqrt(distance))
    vel_x = lax.optimization_barrier(jnp.sum(factor * (source_str[1][None, :] * delta_z - source_str[2][None, :] * delta_y), axis=1))
    vel_y = lax.optimization_barrier(jnp.sum(factor * (source_str[2][None, :] * delta_x - source_str[0][None, :] * delta_z), axis=1))
    vel_z = lax.optimization_barrier(jnp.sum(factor * (source_str[0][None, :] * delta_y - source_str[1][None, :] * delta_x), axis=1))
    return jnp.stack([vel_x, vel_y, vel_z])

def near_blocks(slot_pos, slot_str, member, reach_map):
    slots_total = slot_pos.shape[1]
    block_rows = min(512, slots_total)
    block_count = slots_total // block_rows
    target_pos = slot_pos.reshape(3, block_count, block_rows).transpose(1, 0, 2)
    target_hits = member.reshape(member.shape[0], block_count, block_rows).transpose(1, 0, 2)

    def one_block(block_args):
        block_pos, block_hits = block_args
        pair_mask = lax.dot_general(block_hits, reach_map, (((0,), (0,)), ((), ())), precision=lax.Precision.HIGHEST)
        return near_field(block_pos, slot_pos, slot_str, pair_mask)
    result = lax.map(one_block, (target_pos, target_hits))
    return result.transpose(1, 0, 2).reshape(3, slots_total)

def reference(position, strength, node_box, box_order, box_center, near_list, m2l_source, m2l_type, basis_dir, basis_freq, basis_phase, translation):
    largest_level = lax.Precision.HIGHEST
    groups = N_AGE * N_BOX
    slots_total = 2 * NODE_DEV
    node_count = position.shape[1]
    slot_of_box = jnp.zeros((BOXES,), jnp.int32).at[box_order].set(jnp.arange(BOXES, dtype=jnp.int32))
    node_slot = slot_of_box[node_box]
    owner = (node_slot // BOX_DEV).astype(jnp.int32)
    sorted_idx = jnp.argsort(owner, stable=True).astype(jnp.int32)
    sorted_owner = owner[sorted_idx]
    group_sizes = jnp.zeros((groups,), jnp.int32).at[owner].add(1)
    group_starts = (jnp.cumsum(group_sizes) - group_sizes).astype(jnp.int32)
    rank_within = (jnp.arange(node_count, dtype=jnp.int32) - group_starts[sorted_owner]).astype(jnp.int32)
    slot_table = jnp.full((groups, slots_total), node_count, jnp.int32).at[sorted_owner, rank_within].set(sorted_idx)
    pos_pad = jnp.concatenate([position, jnp.zeros((3, 1), jnp.float32)], axis=1)
    str_pad = jnp.concatenate([strength, jnp.zeros((3, 1), jnp.float32)], axis=1)
    box_pad = jnp.concatenate([node_box, jnp.full((1,), -1, jnp.int32)])

    def group_inputs(group_idx):
        node_index = slot_table[group_idx]
        slot_pos = pos_pad[:, node_index]
        slot_str = str_pad[:, node_index]
        slot_box = box_pad[node_index]
        first_box = (group_idx * BOX_DEV).astype(jnp.int32)
        local_ids = lax.dynamic_slice_in_dim(box_order, first_box, BOX_DEV)
        member = (slot_box[None, :] == local_ids[:, None]).astype(jnp.float32)
        centers = lax.dynamic_slice_in_dim(box_center, first_box, BOX_DEV, 1)
        offsets = slot_pos - jnp.dot(centers, member, precision=largest_level)
        wave_vals, weight = expansion(offsets, slot_str, basis_dir, basis_freq, basis_phase)
        return (slot_pos, slot_str, local_ids, member, wave_vals, weight)

    def group_blocks(group_idx):
        slot_pos, slot_str, local_ids, member, wave_vals, weight = group_inputs(group_idx)
        return lax.dot_general(member, wave_vals * weight, (((1,), (1,)), ((), ())), precision=largest_level)
    blocks = lax.map(group_blocks, jnp.arange(groups, dtype=jnp.int32)).reshape(BOXES, COEF).astype(jnp.bfloat16)
    source_slot = slot_of_box[m2l_source]
    picked = blocks[source_slot].astype(jnp.float32)
    kind_hits = (m2l_type[:, :, None] == jnp.arange(TYPES, dtype=jnp.int32)[None, None, :]).astype(jnp.float32)
    mixed_blocks = jnp.einsum('plt,plc->ptc', kind_hits, picked, precision=largest_level).astype(jnp.bfloat16)
    expansions = jnp.einsum('ptc,tkc->pk', mixed_blocks.astype(jnp.float32), translation.astype(jnp.float32), precision=largest_level)

    def group_velocity(group_idx):
        slot_pos, slot_str, local_ids, member, wave_vals, weight = group_inputs(group_idx)
        first_box = (group_idx * BOX_DEV).astype(jnp.int32)
        near_rows = lax.dynamic_slice_in_dim(near_list, first_box, BOX_DEV, 0)
        allowed = jnp.any(near_rows[:, :, None] == local_ids[None, None, :], axis=1).astype(jnp.float32)
        reach_map = jnp.dot(allowed, member, precision=largest_level)
        near_vel = near_blocks(slot_pos, slot_str, member, reach_map)
        group_exp = lax.dynamic_slice_in_dim(expansions, first_box, BOX_DEV, 0)
        slot_position_here = jnp.dot(group_exp.T, member, precision=largest_level)
        far_vel = jnp.dot(basis_dir, wave_vals * slot_position_here, precision=largest_level)
        return near_vel + far_vel
    velocities = lax.map(group_velocity, jnp.arange(groups, dtype=jnp.int32))
    spread = velocities.transpose(1, 0, 2).reshape(3, groups * slots_total)
    result = jnp.zeros((3, node_count + 1), jnp.float32).at[:, slot_table.reshape(-1)].set(spread)
    return result[:, :node_count]
```

```python
import functools

import jax
import jax.numpy as jnp
import numpy as np
from jax import lax
from jax.experimental import pallas as pl
from jax.experimental.pallas import tpu as pltpu
from jax.sharding import PartitionSpec as P

AXES = ("age", "box")
MESH = pl.DeviceIdType.MESH
core_square = 0.01
inv_four_pi = 0.07957747154594767
inv_two_pi = 0.15915494309189535
LANES = 128
WIDE = 256
VMEM_LIMIT = 56 * 1024 * 1024
f32, bf16, i32 = jnp.float32, jnp.bfloat16, jnp.int32
NN = (((1,), (0,)), ((), ()))
NT = (((1,), (1,)), ((), ()))


def cos_coefficients(degree):
    nodes = np.cos(np.pi * (np.arange(64) + 0.5) / 64)
    w = 0.125 * (nodes + 1.0)
    fit = np.polynomial.chebyshev.Chebyshev.fit(
        w, np.cos(2 * np.pi * np.sqrt(w)), degree, domain=[0, 0.25]
    )
    return [float(c) for c in fit.convert(kind=np.polynomial.Polynomial).coef]


COS_COEF = cos_coefficients(6)


def cos_turns(turns):
    v = turns - ((turns + 12582912.0) - 12582912.0)
    w = v * v
    acc = jnp.full_like(w, COS_COEF[-1])
    for c in COS_COEF[-2::-1]:
        acc = acc * w + c
    return acc


def dot(a, b, dims=NN):
    return lax.dot_general(a, b, dims, preferred_element_type=f32)


def sublane(rows, n):
    return lax.broadcasted_iota(i32, (rows, n), 0)


def hot(row, rows, start=0):
    steps = (sublane(rows, row.shape[1]) + start).astype(f32).astype(bf16)
    return jnp.where(row.astype(bf16) == steps, jnp.ones((), bf16), jnp.zeros((), bf16))


def pieces(x, count):
    out = []
    for _ in range(count):
        piece = x.astype(bf16).astype(f32)
        out.append(piece)
        x = x - piece
    return out


def two(x):
    return jnp.concatenate(pieces(x, 2), axis=0).astype(bf16)


def cross_parts(a, b):
    return (
        a[1:2] * b[2:3] - a[2:3] * b[1:2],
        a[2:3] * b[0:1] - a[0:1] * b[2:3],
        a[0:1] * b[1:2] - a[1:2] * b[0:1],
    )


def before_table():
    row = sublane(LANES, 2 * LANES)
    col = lax.broadcasted_iota(i32, (LANES, 2 * LANES), 1)
    return jnp.where((row < col) | (col >= LANES), 1.0, 0.0).astype(bf16)


def ranks(hits, before, carry):
    kinds = hits[0].shape[0]
    sums = dot(jnp.concatenate([h.astype(bf16) for h in hits], axis=0), before)
    out = []
    for k, h in enumerate(hits):
        part = sums[k * kinds : (k + 1) * kinds]
        out.append(jnp.sum(h * (part[:, :LANES] + carry), axis=0, keepdims=True))
        carry = carry + part[:, LANES:]
    return out, carry


class Sizes:
    def __init__(self, n_age, n_box, nodes, boxes, coef, kinds, entries, near):
        self.n_age, self.n_box, self.nodes, self.boxes = n_age, n_box, nodes, boxes
        self.coef, self.kinds, self.entries, self.near = coef, kinds, entries, near
        self.groups = n_age * n_box
        self.box_total = self.groups * boxes
        self.digits = self.box_total // 32
        self.slots = 2 * nodes
        self.per_peer = self.slots // self.groups
        self.per_box = self.slots // boxes
        self.per_chunk = WIDE // self.per_peer
        self.chunks = self.slots // WIDE
        self.batch = min(8, self.chunks)


def body(
    z,
    pos, stg, node_box, order, center, near_t, source_t, kind, direction, freq, phase, translation,
    out,
    order_own, order_all, order_row, pay, recv, blocks, back, returned,
    near_vm, near_sm, trans, fields, hot_src, owner_row, a_buf, hot_dst, label_dst,
    grouped, lanes, parts, src_tab, tgt_tab, freq_t, wave_hi, wave_lo, sums_f, counts, mixed,
    near_vel, vel, local_sem, order_sem, node_sem, block_sem, back_sem,
):
    groups, n_box, n_age = z.groups, z.n_box, z.n_age
    me_age, me_box = lax.axis_index("age"), lax.axis_index("box")
    me = me_age * n_box + me_box
    barrier = pltpu.get_barrier_semaphore()

    def place(other):
        return {"age": other // n_box, "box": lax.rem(other, n_box)}

    def ahead(d):
        return lax.rem(me + d, groups)

    def behind(d):
        return lax.rem(me + groups - d, groups)

    def loop(lo, hi, f):
        def step(i, carry):
            f(i)
            return carry

        lax.fori_loop(lo, hi, step, 0)

    loop(
        1, groups,
        lambda d: pl.semaphore_signal(
            barrier, inc=1, device_id=place(ahead(d)), device_id_type=MESH
        ),
    )
    load_translation = pltpu.make_async_copy(translation, trans, local_sem.at[0])
    load_translation.start()
    order_own[...] = jnp.full((1, LANES), -1, i32)
    order_own[:, : z.boxes] = order[...]
    order_all[me] = order_own[...]
    pl.semaphore_wait(barrier, groups - 1)

    def order_copy(d):
        return pltpu.make_async_remote_copy(
            src_ref=order_own,
            dst_ref=order_all.at[me],
            send_sem=order_sem.at[0, d - 1],
            recv_sem=order_sem.at[1, d - 1],
            device_id=place(ahead(d)),
            device_id_type=MESH,
        )

    loop(1, groups, lambda d: order_copy(d).start())

    waves = jnp.concatenate(
        [freq[...], phase[...], jnp.zeros((4, z.coef), f32)], axis=0
    ) * inv_two_pi
    f1, f2, f3 = pieces(waves, 3)
    table = jnp.concatenate(
        [f1, f2, f1, f3, f2, f1, jnp.zeros((LANES - 48, z.coef), f32)], axis=0
    )
    freq_t[...] = table.T[:, :48].astype(bf16)
    before = before_table()

    loop(1, groups, lambda d: order_copy(d).wait())

    m = LANES // z.boxes
    lane8 = lax.broadcasted_iota(i32, (8, LANES), 1)
    for t in range(z.box_total // LANES):
        tile = jnp.broadcast_to(order_all[t * m], (8, LANES))
        for u in range(1, m):
            shifted = pltpu.roll(
                jnp.broadcast_to(order_all[t * m + u], (8, LANES)), u * z.boxes, 1
            )
            tile = jnp.where(lane8 >= u * z.boxes, shifted, tile)
        order_row[:, t * LANES : (t + 1) * LANES] = tile
    ids = order_row[0:1, :]
    at = lax.broadcasted_iota(i32, (1, z.box_total), 1)
    high_hot = sublane(z.digits, z.box_total) == (ids >> 5)
    owner_of = (at // z.boxes).astype(f32)
    label_of = lax.rem(at, z.boxes).astype(f32)
    finder = dot(
        jnp.concatenate(
            [jnp.where(high_hot, owner_of, 0.0), jnp.where(high_hot, label_of, 0.0)], axis=0
        ).astype(bf16),
        hot((ids & 31).astype(f32), 32),
        NT,
    ).astype(bf16)

    def find(box_ids):
        got = dot(finder, hot((box_ids & 31).astype(f32), 32))
        mine = sublane(z.digits, box_ids.shape[1]) == (box_ids >> 5)
        who = jnp.sum(jnp.where(mine, got[: z.digits], 0.0), axis=0, keepdims=True)
        label = jnp.sum(jnp.where(mine, got[z.digits :], 0.0), axis=0, keepdims=True)
        return who, label

    step_nodes = min(1024, z.nodes)
    for s in range(z.nodes // step_nodes):
        here = slice(s * step_nodes, (s + 1) * step_nodes)
        who, label = find(node_box[:, here])
        owner_row[:, here] = who
        fields[:, here] = two(
            jnp.concatenate(
                [pos[:, here], stg[:, here], label + 1.0, jnp.zeros_like(label)], axis=0
            )
        )

    hits = []
    for k in range(z.nodes // LANES):
        row = owner_row[:, k * LANES : (k + 1) * LANES]
        hits.append(jnp.where(sublane(groups, LANES).astype(f32) == row, 1.0, 0.0))
    rank, _ = ranks(hits, before, jnp.zeros((groups, LANES), f32))
    hot_src[...] = hot(jnp.concatenate(rank, axis=1), z.per_peer)

    near_ids = near_t[...]
    for v in range(z.near):
        row = near_ids[v : v + 1]
        _, label = find(row)
        near_vm[v : v + 1, : z.boxes] = jnp.where(row >= 0, label.astype(i32), z.boxes)
    near_copy = pltpu.make_async_copy(near_vm, near_sm, local_sem.at[1])
    near_copy.start()

    def node_copy(d):
        return pltpu.make_async_remote_copy(
            src_ref=pay.at[ahead(d)],
            dst_ref=recv.at[me],
            send_sem=node_sem.at[0, d - 1],
            recv_sem=node_sem.at[1, d - 1],
            device_id=place(ahead(d)),
            device_id_type=MESH,
        )

    per_step = min(8, groups)

    def make_payload(k):
        owners = owner_row[...].astype(bf16)
        f = fields[...]
        rows = []
        for u in range(per_step):
            g = ahead(1 + k * per_step + u)
            g16 = jnp.full((1, LANES), g, i32).astype(f32).astype(bf16)[:, :1]
            rows.append(jnp.where(owners == g16, f, jnp.zeros((), bf16)))
        made = dot(jnp.concatenate(rows, axis=0), hot_src[...], NT)
        for u in range(per_step):
            d = 1 + k * per_step + u
            pay[ahead(d)] = made[16 * u : 16 * u + 8] + made[16 * u + 8 : 16 * u + 16]

            @pl.when(d < groups)
            def _():
                node_copy(d).start()

    loop(0, groups // per_step, make_payload)
    recv[me] = pay[me]

    for j in range(z.boxes):
        from_box = jnp.where(source_t[:, j : j + 1] == ids, 1.0, 0.0).astype(bf16)
        of_kind = jnp.where(
            kind[j : j + 1, :] == sublane(z.kinds, z.entries), 1.0, 0.0
        ).astype(bf16)
        counts[z.kinds * j : z.kinds * (j + 1), :] = dot(of_kind, from_box).astype(bf16)

    def load_chunk(ref, c):
        parts_ = [ref[behind(c * z.per_chunk + v)] for v in range(z.per_chunk)]
        return parts_[0] if z.per_chunk == 1 else jnp.concatenate(parts_, axis=1)

    grouped[...] = jnp.zeros_like(grouped)

    def group_batch(t, carry):
        def arrive(d, c):
            @pl.when(d > 0)
            def _():
                node_copy(d).wait()

            return c

        first = t * z.batch * z.per_chunk
        lax.fori_loop(first, first + z.batch * z.per_chunk, arrive, 0)
        labels, hits, tables = [], [], []
        for u in range(z.batch):
            blk = load_chunk(recv, t * z.batch + u)
            label = blk[6:7]
            label_dst[t * z.batch + u] = label
            labels.append(label)
            tables.append(two(blk))
            for h in range(WIDE // LANES):
                part = label[:, h * LANES : (h + 1) * LANES]
                hits.append(
                    jnp.where((sublane(z.boxes, LANES) + 1).astype(f32) == part, 1.0, 0.0)
                )
        rank, carry = ranks(hits, before_table(), carry)
        per = WIDE // LANES
        for u in range(z.batch):
            row = jnp.concatenate(rank[u * per : (u + 1) * per], axis=1)
            row = jnp.where(labels[u] > 0.0, row, -1.0)
            cols = slice(u * WIDE, (u + 1) * WIDE)
            hot_dst[t, :, cols] = hot(row, z.per_box)
            label16 = labels[u].astype(bf16)
            for b in range(z.boxes):
                a_buf[16 * b : 16 * b + 16, cols] = jnp.where(
                    label16 == jnp.full((), b + 1, bf16), tables[u], jnp.zeros((), bf16)
                )
        grouped[...] += dot(a_buf[...], hot_dst[t], NT)
        return carry

    lax.fori_loop(0, z.chunks // z.batch, group_batch, jnp.zeros((z.boxes, LANES), f32))

    def box_waves(b):
        got = grouped[pl.ds(pl.multiple_of(16 * b, 16), 16), :]
        lan = got[0:8] + got[8:16]
        lanes[b] = lan
        p, s = lan[0:3], lan[3:6]
        n = z.per_box
        zero = jnp.zeros((1, n), f32)
        one = jnp.ones((1, n), f32)
        part = two(jnp.concatenate([s, zero, *cross_parts(s, p), zero], axis=0))
        parts[b] = part
        p1, p2 = got[0:3], got[8:11]
        square = p[0:1] * p[0:1] + p[1:2] * p[1:2] + p[2:3] * p[2:3]
        pad = jnp.zeros((14, n), f32)
        tgt_tab[b] = jnp.concatenate(
            [p1, p1, p2, p2, one, one, one, *pieces(square + core_square, 3), pad], axis=0
        ).astype(bf16)
        src = jnp.concatenate(
            [-2.0 * p1, -2.0 * p2, -2.0 * p1, -2.0 * p2, *pieces(square, 3), one, one, one,
             jnp.zeros((LANES - 18, n), f32)],
            axis=0,
        )
        src_tab[b] = src.T[:, :32].astype(bf16)
        o1, o2, o3 = pieces(
            jnp.concatenate(
                [p[0:1] - center[0, b], p[1:2] - center[1, b], p[2:3] - center[2, b], one,
                 jnp.zeros((4, n), f32)],
                axis=0,
            ),
            3,
        )
        stacked = jnp.concatenate([o3, o2, o2, o1, o1, o1], axis=0).astype(bf16)
        turns = dot(freq_t[...], stacked)
        rows = 32
        highs, lows = [], []
        for c in range(z.coef // rows):
            wave = cos_turns(turns[c * rows : (c + 1) * rows])
            high = wave.astype(bf16)
            highs.append(high)
            lows.append((wave - high.astype(f32)).astype(bf16))
        high = jnp.concatenate(highs, axis=0)
        low = jnp.concatenate(lows, axis=0)
        wave_hi[b] = high
        wave_lo[b] = low
        sums = dot(part, high, NT) + dot(part, low, NT)
        sums = sums[0:8] + sums[8:16]
        sums_f[pl.ds(b, 1), :] = (
            direction[0:1, :] * sums[0:1]
            + direction[1:2, :] * sums[1:2]
            + direction[2:3, :] * sums[2:3]
        )

    loop(0, z.boxes, box_waves)
    parts[z.boxes] = jnp.zeros_like(parts[z.boxes])
    lane32 = lax.broadcasted_iota(i32, (z.per_box, 32), 1)
    src_tab[z.boxes] = jnp.where((lane32 >= 15) & (lane32 < 18), 1.0, 0.0).astype(bf16)
    near_copy.wait()

    blocks[me_age, me_box] = sums_f[...].astype(bf16)

    def along_box(d):
        return pltpu.make_async_remote_copy(
            src_ref=blocks.at[me_age, me_box],
            dst_ref=blocks.at[me_age, me_box],
            send_sem=block_sem.at[0, d - 1],
            recv_sem=block_sem.at[1, d - 1],
            device_id={"age": me_age, "box": lax.rem(me_box + d, n_box)},
            device_id_type=MESH,
        )

    def along_age(d):
        return pltpu.make_async_remote_copy(
            src_ref=blocks.at[me_age],
            dst_ref=blocks.at[me_age],
            send_sem=block_sem.at[0, n_box - 2 + d],
            recv_sem=block_sem.at[1, n_box - 2 + d],
            device_id={"age": lax.rem(me_age + d, n_age), "box": me_box},
            device_id_type=MESH,
        )

    def near_box(b):
        sums = jnp.zeros((16, z.per_box), f32)
        target = tgt_tab[b]
        for v in range(z.near):
            j = jnp.clip(near_sm[v, b], 0, z.boxes)
            r = lax.rsqrt(dot(src_tab[j], target))
            sums = sums + dot(parts[j], (r * r * r).astype(bf16))
        sums = sums[0:8] + sums[8:16]
        at_b = lanes[b]
        pad = jnp.zeros((5, z.per_box), f32)
        near = jnp.concatenate([*cross_parts(sums[0:3], at_b[0:3]), pad], axis=0)
        near_vel[b] = (near - jnp.concatenate([sums[4:7], pad], axis=0)) * inv_four_pi

    first = z.boxes // 4
    loop(1, n_box, lambda d: along_box(d).start())
    loop(0, first, near_box)
    loop(1, n_box, lambda d: along_box(d).wait())
    loop(1, n_age, lambda d: along_age(d).start())
    loop(first, z.boxes, near_box)
    loop(1, n_age, lambda d: along_age(d).wait())
    load_translation.wait()

    every = dot(counts[...], blocks[...].reshape(z.box_total, z.coef))
    for h in range(z.coef // LANES):
        mixed[h] = every[:, h * LANES : (h + 1) * LANES]
    expansion = jnp.zeros((z.boxes, z.coef), f32)
    for t in range(z.kinds):
        rows = [mixed[h, pl.ds(t, z.boxes, stride=z.kinds), :] for h in range(z.coef // LANES)]
        expansion = expansion + dot(jnp.concatenate(rows, axis=1).astype(bf16), trans[t], NT)
    sums_f[...] = expansion

    def far_box(b):
        row = sums_f[pl.ds(b, 1), :]
        table = two(
            jnp.concatenate([direction[...] * row, jnp.zeros((5, z.coef), f32)], axis=0)
        )
        far = dot(table, wave_hi[b]) + dot(table, wave_lo[b])
        total = near_vel[b] + far[0:8] + far[8:16]
        v1, v2 = pieces(total[0:3], 2)
        vel[pl.ds(pl.multiple_of(8 * b, 8), 8), :] = jnp.concatenate(
            [v1, v2, jnp.zeros((2, z.per_box), f32)], axis=0
        )

    loop(0, z.boxes, far_box)

    def back_copy(d):
        return pltpu.make_async_remote_copy(
            src_ref=back.at[behind(d)],
            dst_ref=returned.at[me],
            send_sem=back_sem.at[0, d - 1],
            recv_sem=back_sem.at[1, d - 1],
            device_id=place(behind(d)),
            device_id_type=MESH,
        )

    def pick(made, row, kinds, start):
        total = jnp.zeros((8, row.shape[1]), f32)
        for k in range(kinds):
            total = total + jnp.where(row == float(k + start), made[8 * k : 8 * k + 8], 0.0)
        return total[0:3] + total[3:6]

    per_chunk = z.per_chunk

    def send_back(t):
        table = vel[...].astype(bf16)
        for u in range(z.batch):
            c = t * z.batch + u
            made = dot(table, hot_dst[t, :, u * WIDE : (u + 1) * WIDE])
            done = pick(made, label_dst[c], z.boxes, 1)
            for v in range(per_chunk):
                d = c * per_chunk + v
                back[behind(d)] = done[:, v * z.per_peer : (v + 1) * z.per_peer]

                @pl.when(d > 0)
                def _():
                    back_copy(d).start()

    loop(0, z.chunks // z.batch, send_back)
    returned[me] = back[me]
    loop(1, groups, lambda d: back_copy(d).wait())

    rows = []
    for g in range(groups):
        v1, v2 = pieces(returned[g], 2)
        rows.append(jnp.concatenate([v1, v2, jnp.zeros((2, z.per_peer), f32)], axis=0))
    table = jnp.concatenate(rows, axis=0).astype(bf16)
    for s in range(z.nodes // 512):
        here = slice(s * 512, (s + 1) * 512)
        made = dot(table, hot_src[:, here])
        out[:, here] = pick(made, owner_row[:, here], groups, 0)


def per_device(
    n_age,
    n_box,
    position,
    strength,
    node_box,
    box_order,
    box_center,
    near_list,
    m2l_source,
    m2l_type,
    basis_dir,
    basis_freq,
    basis_phase,
    translation,
):
    z = Sizes(
        n_age, n_box, position.shape[1], box_order.shape[0], basis_phase.shape[0],
        translation.shape[0], m2l_source.shape[1], near_list.shape[1],
    )
    vm = pl.BlockSpec(memory_space=pltpu.VMEM)
    sm = pl.BlockSpec(memory_space=pltpu.SMEM)
    dma = pltpu.SemaphoreType.DMA

    def buf(shape, dtype=f32):
        return pltpu.VMEM(shape, dtype)

    return pl.pallas_call(
        functools.partial(body, z),
        out_shape=jax.ShapeDtypeStruct((3, z.nodes), f32),
        in_specs=[vm, vm, vm, vm, sm, vm, vm, vm, vm, vm, vm, pl.BlockSpec(memory_space=pl.ANY)],
        out_specs=vm,
        scratch_shapes=[
            buf((1, LANES), i32),
            buf((z.groups, 1, LANES), i32),
            buf((8, z.box_total), i32),
            buf((z.groups, 8, z.per_peer)),
            buf((z.groups, 8, z.per_peer)),
            buf((n_age, n_box, z.boxes, z.coef), bf16),
            buf((z.groups, 3, z.per_peer)),
            buf((z.groups, 3, z.per_peer)),
            buf((8, LANES), i32),
            pltpu.SMEM((8, LANES), i32),
            buf(translation.shape, bf16),
            buf((16, z.nodes), bf16),
            buf((z.per_peer, z.nodes), bf16),
            buf((1, z.nodes)),
            buf((16 * z.boxes, z.batch * WIDE), bf16),
            buf((z.chunks // z.batch, z.per_box, z.batch * WIDE), bf16),
            buf((z.chunks, 1, WIDE)),
            buf((16 * z.boxes, z.per_box)),
            buf((z.boxes, 8, z.per_box)),
            buf((z.boxes + 1, 16, z.per_box), bf16),
            buf((z.boxes + 1, z.per_box, 32), bf16),
            buf((z.boxes, 32, z.per_box), bf16),
            buf((z.coef, 48), bf16),
            buf((z.boxes, z.coef, z.per_box), bf16),
            buf((z.boxes, z.coef, z.per_box), bf16),
            buf((z.boxes, z.coef)),
            buf((z.kinds * z.boxes, z.box_total), bf16),
            buf((z.coef // LANES, z.kinds * z.boxes, LANES)),
            buf((z.boxes, 8, z.per_box)),
            buf((8 * z.boxes, z.per_box)),
            dma((2,)),
            dma((2, z.groups - 1)),
            dma((2, z.groups - 1)),
            dma((2, n_age + n_box - 2)),
            dma((2, z.groups - 1)),
        ],
        compiler_params=pltpu.CompilerParams(
            collective_id=0, has_side_effects=True, vmem_limit_bytes=VMEM_LIMIT
        ),
    )(
        position,
        strength,
        node_box.reshape(1, -1),
        box_order.reshape(1, -1),
        box_center,
        near_list.T,
        m2l_source.T,
        m2l_type,
        basis_dir,
        basis_freq,
        basis_phase.reshape(1, -1),
        translation,
    )


def solution(mesh):
    n_box = mesh.shape["box"]
    n_age = mesh.shape["age"]
    placed = (
        P(None, AXES),
        P(None, AXES),
        P(AXES),
        P(AXES),
        P(None, AXES),
        P(AXES, None),
        P(AXES, None),
        P(AXES, None),
        P(),
        P(),
        P(),
        P(),
    )
    return jax.shard_map(
        functools.partial(per_device, n_age, n_box),
        mesh=mesh,
        in_specs=placed,
        out_specs=P(None, AXES),
        check_vma=False,
    )
```

```python
import functools

import jax
import jax.numpy as jnp
import numpy as np
from jax import lax
from jax.experimental import pallas as pl
from jax.experimental.pallas import tpu as pltpu
from jax.sharding import PartitionSpec as P

AXES = ("age", "box")
MESH = pl.DeviceIdType.MESH
core_square = 0.01
inv_four_pi = 0.07957747154594767
inv_two_pi = 0.15915494309189535
LANES = 128
WIDE = 256
VMEM_LIMIT = 56 * 1024 * 1024
f32, bf16, i32 = jnp.float32, jnp.bfloat16, jnp.int32
NN = (((1,), (0,)), ((), ()))
NT = (((1,), (1,)), ((), ()))


def cos_coefficients(degree):
    nodes = np.cos(np.pi * (np.arange(64) + 0.5) / 64)
    w = 0.125 * (nodes + 1.0)
    fit = np.polynomial.chebyshev.Chebyshev.fit(
        w, np.cos(2 * np.pi * np.sqrt(w)), degree, domain=[0, 0.25]
    )
    return [float(c) for c in fit.convert(kind=np.polynomial.Polynomial).coef]


COS_COEF = cos_coefficients(5)


def cos_turns(turns):
    v = turns - ((turns + 12582912.0) - 12582912.0)
    w = v * v
    acc = jnp.full_like(w, COS_COEF[-1])
    for c in COS_COEF[-2::-1]:
        acc = acc * w + c
    return acc


def dot(a, b, dims=NN):
    return lax.dot_general(a, b, dims, preferred_element_type=f32)


def sublane(rows, n):
    return lax.broadcasted_iota(i32, (rows, n), 0)


def hot(row, rows, start=0):
    steps = (sublane(rows, row.shape[1]) + start).astype(f32).astype(bf16)
    return jnp.where(row.astype(bf16) == steps, jnp.ones((), bf16), jnp.zeros((), bf16))


def pieces(x, count):
    out = []
    for _ in range(count):
        piece = x.astype(bf16).astype(f32)
        out.append(piece)
        x = x - piece
    return out


def two(x):
    return jnp.concatenate(pieces(x, 2), axis=0).astype(bf16)


def cross_parts(a, b):
    return (
        a[1:2] * b[2:3] - a[2:3] * b[1:2],
        a[2:3] * b[0:1] - a[0:1] * b[2:3],
        a[0:1] * b[1:2] - a[1:2] * b[0:1],
    )


def before_table():
    row = sublane(LANES, 2 * LANES)
    col = lax.broadcasted_iota(i32, (LANES, 2 * LANES), 1)
    return jnp.where((row < col) | (col >= LANES), 1.0, 0.0).astype(bf16)


def ranks(hits, before, carry):
    kinds = hits[0].shape[0]
    sums = dot(jnp.concatenate([h.astype(bf16) for h in hits], axis=0), before)
    out = []
    for k, h in enumerate(hits):
        part = sums[k * kinds : (k + 1) * kinds]
        out.append(jnp.sum(h * (part[:, :LANES] + carry), axis=0, keepdims=True))
        carry = carry + part[:, LANES:]
    return out, carry


class Sizes:
    def __init__(self, n_age, n_box, nodes, boxes, coef, kinds, entries, near):
        self.n_age, self.n_box, self.nodes, self.boxes = n_age, n_box, nodes, boxes
        self.coef, self.kinds, self.entries, self.near = coef, kinds, entries, near
        self.groups = n_age * n_box
        self.box_total = self.groups * boxes
        self.digits = self.box_total // 32
        self.slots = 2 * nodes
        self.per_peer = self.slots // self.groups
        self.per_box = self.slots // boxes
        self.per_chunk = WIDE // self.per_peer
        self.chunks = self.slots // WIDE
        self.batch = min(8, self.chunks)


def body(
    z,
    pos, stg, node_box, order, center, near_t, source, kind, direction, freq, phase, translation,
    out,
    order_own, order_all, order_row, pay, recv, blocks, back, returned,
    near_vm, near_sm, trans, fields, hot_src, owner_row, a_buf, hot_dst, label_dst,
    grouped, lanes, parts, src_tab, tgt_tab, freq_t, wave_hi, wave_lo, sums_f, counts, mixed,
    near_vel, vel, local_sem, order_sem, node_sem, block_sem, back_sem,
):
    groups, n_box, n_age = z.groups, z.n_box, z.n_age
    me_age, me_box = lax.axis_index("age"), lax.axis_index("box")
    me = me_age * n_box + me_box
    barrier = pltpu.get_barrier_semaphore()

    def place(other):
        return {"age": other // n_box, "box": lax.rem(other, n_box)}

    def ahead(d):
        return lax.rem(me + d, groups)

    def behind(d):
        return lax.rem(me + groups - d, groups)

    def loop(lo, hi, f, unroll=1):
        def step(i, carry):
            f(i)
            return carry

        lax.fori_loop(lo, hi, step, 0, unroll=unroll)

    loop(
        1, groups,
        lambda d: pl.semaphore_signal(
            barrier, inc=1, device_id=place(ahead(d)), device_id_type=MESH
        ),
    )
    load_translation = pltpu.make_async_copy(translation, trans, local_sem.at[0])
    load_translation.start()
    order_own[...] = jnp.full((1, LANES), -1, i32)
    order_own[:, : z.boxes] = order[...]
    order_all[me] = order_own[...]
    pl.semaphore_wait(barrier, groups - 1)

    def order_copy(d):
        return pltpu.make_async_remote_copy(
            src_ref=order_own,
            dst_ref=order_all.at[me],
            send_sem=order_sem.at[0, d - 1],
            recv_sem=order_sem.at[1, d - 1],
            device_id=place(ahead(d)),
            device_id_type=MESH,
        )

    loop(1, groups, lambda d: order_copy(d).start())

    waves = jnp.concatenate(
        [freq[...], phase[...], jnp.zeros((4, z.coef), f32)], axis=0
    ) * inv_two_pi
    f1, f2, f3 = pieces(waves, 3)
    table = jnp.concatenate(
        [f1, f2, f1, f3, f2, f1, jnp.zeros((LANES - 48, z.coef), f32)], axis=0
    )
    freq_t[...] = table.T[:, :48].astype(bf16)
    before = before_table()

    loop(1, groups, lambda d: order_copy(d).wait())

    m = LANES // z.boxes
    lane8 = lax.broadcasted_iota(i32, (8, LANES), 1)
    for t in range(z.box_total // LANES):
        tile = jnp.broadcast_to(order_all[t * m], (8, LANES))
        for u in range(1, m):
            shifted = pltpu.roll(
                jnp.broadcast_to(order_all[t * m + u], (8, LANES)), u * z.boxes, 1
            )
            tile = jnp.where(lane8 >= u * z.boxes, shifted, tile)
        order_row[:, t * LANES : (t + 1) * LANES] = tile
    ids = order_row[0:1, :]
    at = lax.broadcasted_iota(i32, (1, z.box_total), 1)
    high_hot = sublane(z.digits, z.box_total) == (ids >> 5)
    owner_of = (at // z.boxes).astype(f32)
    label_of = lax.rem(at, z.boxes).astype(f32)
    finder = dot(
        jnp.concatenate(
            [jnp.where(high_hot, owner_of, 0.0), jnp.where(high_hot, label_of, 0.0)], axis=0
        ).astype(bf16),
        hot((ids & 31).astype(f32), 32),
        NT,
    ).astype(bf16)

    def find(box_ids):
        got = dot(finder, hot((box_ids & 31).astype(f32), 32))
        mine = sublane(z.digits, box_ids.shape[1]) == (box_ids >> 5)
        who = jnp.sum(jnp.where(mine, got[: z.digits], 0.0), axis=0, keepdims=True)
        label = jnp.sum(jnp.where(mine, got[z.digits :], 0.0), axis=0, keepdims=True)
        return who, label

    step_nodes = min(1024, z.nodes)
    for s in range(z.nodes // step_nodes):
        here = slice(s * step_nodes, (s + 1) * step_nodes)
        who, label = find(node_box[:, here])
        owner_row[:, here] = who
        fields[:, here] = two(
            jnp.concatenate(
                [pos[:, here], stg[:, here], label + 1.0, jnp.zeros_like(label)], axis=0
            )
        )

    hits = []
    for k in range(z.nodes // LANES):
        row = owner_row[:, k * LANES : (k + 1) * LANES]
        hits.append(jnp.where(sublane(groups, LANES).astype(f32) == row, 1.0, 0.0))
    rank, _ = ranks(hits, before, jnp.zeros((groups, LANES), f32))
    hot_src[...] = hot(jnp.concatenate(rank, axis=1), z.per_peer)

    near_ids = near_t[...]
    for v in range(z.near):
        row = near_ids[v : v + 1]
        _, label = find(row)
        near_vm[v : v + 1, : z.boxes] = jnp.where(row >= 0, label.astype(i32), z.boxes)
    near_copy = pltpu.make_async_copy(near_vm, near_sm, local_sem.at[1])
    near_copy.start()

    def node_copy(d):
        return pltpu.make_async_remote_copy(
            src_ref=pay.at[ahead(d)],
            dst_ref=recv.at[me],
            send_sem=node_sem.at[0, d - 1],
            recv_sem=node_sem.at[1, d - 1],
            device_id=place(ahead(d)),
            device_id_type=MESH,
        )

    per_step = min(8, groups)

    def make_payload(k):
        owners = owner_row[...].astype(bf16)
        f = fields[...]
        rows = []
        for u in range(per_step):
            g = ahead(1 + k * per_step + u)
            g16 = jnp.full((1, LANES), g, i32).astype(f32).astype(bf16)[:, :1]
            rows.append(jnp.where(owners == g16, f, jnp.zeros((), bf16)))
        made = dot(jnp.concatenate(rows, axis=0), hot_src[...], NT)
        for u in range(per_step):
            d = 1 + k * per_step + u
            pay[ahead(d)] = made[16 * u : 16 * u + 8] + made[16 * u + 8 : 16 * u + 16]
        start = 1 + k * per_step
        loop(start, jnp.minimum(start + per_step, groups), lambda d: node_copy(d).start())

    loop(0, groups // per_step, make_payload)
    recv[me] = pay[me]

    square = jnp.concatenate(
        [source[...], jnp.zeros((z.boxes, LANES - z.entries), i32)], axis=1
    ).astype(f32)
    square = jnp.concatenate([square, jnp.zeros((LANES - z.boxes, LANES), f32)], axis=0)
    source_t = square.T[: z.entries].astype(i32)
    for j in range(z.boxes):
        from_box = jnp.where(source_t[:, j : j + 1] == ids, 1.0, 0.0).astype(bf16)
        of_kind = jnp.where(
            kind[j : j + 1, :] == sublane(z.kinds, z.entries), 1.0, 0.0
        ).astype(bf16)
        counts[z.kinds * j : z.kinds * (j + 1), :] = dot(of_kind, from_box).astype(bf16)

    def load_chunk(ref, c):
        parts_ = [ref[behind(c * z.per_chunk + v)] for v in range(z.per_chunk)]
        return parts_[0] if z.per_chunk == 1 else jnp.concatenate(parts_, axis=1)

    grouped[...] = jnp.zeros_like(grouped)

    def group_batch(t, carry):
        def arrive(d, c):
            @pl.when(d > 0)
            def _():
                node_copy(d).wait()

            return c

        first = t * z.batch * z.per_chunk
        lax.fori_loop(first, first + z.batch * z.per_chunk, arrive, 0)
        labels, hits, tables = [], [], []
        for u in range(z.batch):
            blk = load_chunk(recv, t * z.batch + u)
            label = blk[6:7]
            label_dst[t * z.batch + u] = label
            labels.append(label)
            tables.append(two(blk))
            for h in range(WIDE // LANES):
                part = label[:, h * LANES : (h + 1) * LANES]
                hits.append(
                    jnp.where((sublane(z.boxes, LANES) + 1).astype(f32) == part, 1.0, 0.0)
                )
        rank, carry = ranks(hits, before_table(), carry)
        per = WIDE // LANES
        for u in range(z.batch):
            row = jnp.concatenate(rank[u * per : (u + 1) * per], axis=1)
            row = jnp.where(labels[u] > 0.0, row, -1.0)
            cols = slice(u * WIDE, (u + 1) * WIDE)
            hot_dst[t, :, cols] = hot(row, z.per_box)
            label16 = labels[u].astype(bf16)
            for b in range(z.boxes):
                a_buf[16 * b : 16 * b + 16, cols] = jnp.where(
                    label16 == jnp.full((), b + 1, bf16), tables[u], jnp.zeros((), bf16)
                )
        grouped[...] += dot(a_buf[...], hot_dst[t], NT)
        return carry

    lax.fori_loop(0, z.chunks // z.batch, group_batch, jnp.zeros((z.boxes, LANES), f32))

    def box_waves(b):
        got = grouped[pl.ds(pl.multiple_of(16 * b, 16), 16), :]
        lan = got[0:8] + got[8:16]
        lanes[b] = lan
        p, s = lan[0:3], lan[3:6]
        n = z.per_box
        zero = jnp.zeros((1, n), f32)
        one = jnp.ones((1, n), f32)
        part = two(jnp.concatenate([s, zero, *cross_parts(s, p), zero], axis=0))
        parts[b] = part
        p1, p2 = got[0:3], got[8:11]
        square = p[0:1] * p[0:1] + p[1:2] * p[1:2] + p[2:3] * p[2:3]
        pad = jnp.zeros((14, n), f32)
        tgt_tab[b] = jnp.concatenate(
            [p1, p1, p2, p2, one, one, one, *pieces(square + core_square, 3), pad], axis=0
        ).astype(bf16)
        src = jnp.concatenate(
            [-2.0 * p1, -2.0 * p2, -2.0 * p1, -2.0 * p2, *pieces(square, 3), one, one, one,
             jnp.zeros((LANES - 18, n), f32)],
            axis=0,
        )
        src_tab[b] = src.T[:, :32].astype(bf16)
        o1, o2, o3 = pieces(
            jnp.concatenate(
                [p[0:1] - center[0, b], p[1:2] - center[1, b], p[2:3] - center[2, b], one,
                 jnp.zeros((4, n), f32)],
                axis=0,
            ),
            3,
        )
        stacked = jnp.concatenate([o3, o2, o2, o1, o1, o1], axis=0).astype(bf16)
        turns = dot(freq_t[...], stacked)
        rows = 32
        highs, lows = [], []
        for c in range(z.coef // rows):
            wave = cos_turns(turns[c * rows : (c + 1) * rows])
            high = wave.astype(bf16)
            highs.append(high)
            lows.append((wave - high.astype(f32)).astype(bf16))
        high = jnp.concatenate(highs, axis=0)
        low = jnp.concatenate(lows, axis=0)
        wave_hi[b] = high
        wave_lo[b] = low
        sums = dot(part, high, NT) + dot(part, low, NT)
        sums = sums[0:8] + sums[8:16]
        sums_f[pl.ds(b, 1), :] = (
            direction[0:1, :] * sums[0:1]
            + direction[1:2, :] * sums[1:2]
            + direction[2:3, :] * sums[2:3]
        )

    loop(0, z.boxes, box_waves, 4)
    parts[z.boxes] = jnp.zeros_like(parts[z.boxes])
    lane32 = lax.broadcasted_iota(i32, (z.per_box, 32), 1)
    src_tab[z.boxes] = jnp.where((lane32 >= 15) & (lane32 < 18), 1.0, 0.0).astype(bf16)
    near_copy.wait()

    blocks[me_age, me_box] = sums_f[...].astype(bf16)

    def along_box(d):
        return pltpu.make_async_remote_copy(
            src_ref=blocks.at[me_age, me_box],
            dst_ref=blocks.at[me_age, me_box],
            send_sem=block_sem.at[0, d - 1],
            recv_sem=block_sem.at[1, d - 1],
            device_id={"age": me_age, "box": lax.rem(me_box + d, n_box)},
            device_id_type=MESH,
        )

    def along_age(d):
        return pltpu.make_async_remote_copy(
            src_ref=blocks.at[me_age],
            dst_ref=blocks.at[me_age],
            send_sem=block_sem.at[0, n_box - 2 + d],
            recv_sem=block_sem.at[1, n_box - 2 + d],
            device_id={"age": lax.rem(me_age + d, n_age), "box": me_box},
            device_id_type=MESH,
        )

    def near_box(b):
        sums = jnp.zeros((16, z.per_box), f32)
        target = tgt_tab[b]
        for first_v in range(0, z.near, 2):
            picks = [
                jnp.clip(near_sm[v, b], 0, z.boxes) for v in range(first_v, min(first_v + 2, z.near))
            ]
            factors = []
            for j in picks:
                r = lax.rsqrt(dot(src_tab[j], target))
                factors.append((r * r * r).astype(bf16))
            for j, factor in zip(picks, factors):
                sums = sums + dot(parts[j], factor)
        sums = sums[0:8] + sums[8:16]
        at_b = lanes[b]
        pad = jnp.zeros((5, z.per_box), f32)
        near = jnp.concatenate([*cross_parts(sums[0:3], at_b[0:3]), pad], axis=0)
        near_vel[b] = (near - jnp.concatenate([sums[4:7], pad], axis=0)) * inv_four_pi

    first = z.boxes // 4
    loop(1, n_box, lambda d: along_box(d).start())
    loop(0, first, near_box, 2)
    loop(1, n_box, lambda d: along_box(d).wait())
    loop(1, n_age, lambda d: along_age(d).start())
    loop(first, z.boxes, near_box, 2)
    loop(1, n_age, lambda d: along_age(d).wait())
    load_translation.wait()

    every = dot(counts[...], blocks[...].reshape(z.box_total, z.coef))
    for h in range(z.coef // LANES):
        mixed[h] = every[:, h * LANES : (h + 1) * LANES]
    expansion = jnp.zeros((z.boxes, z.coef), f32)
    for t in range(z.kinds):
        rows = [mixed[h, pl.ds(t, z.boxes, stride=z.kinds), :] for h in range(z.coef // LANES)]
        expansion = expansion + dot(jnp.concatenate(rows, axis=1).astype(bf16), trans[t], NT)
    sums_f[...] = expansion

    def far_box(b):
        row = sums_f[pl.ds(b, 1), :]
        table = two(
            jnp.concatenate([direction[...] * row, jnp.zeros((5, z.coef), f32)], axis=0)
        )
        far = dot(table, wave_hi[b]) + dot(table, wave_lo[b])
        total = near_vel[b] + far[0:8] + far[8:16]
        v1, v2 = pieces(total[0:3], 2)
        vel[pl.ds(pl.multiple_of(8 * b, 8), 8), :] = jnp.concatenate(
            [v1, v2, jnp.zeros((2, z.per_box), f32)], axis=0
        )

    loop(0, z.boxes, far_box, 8)

    def back_copy(d):
        return pltpu.make_async_remote_copy(
            src_ref=back.at[behind(d)],
            dst_ref=returned.at[me],
            send_sem=back_sem.at[0, d - 1],
            recv_sem=back_sem.at[1, d - 1],
            device_id=place(behind(d)),
            device_id_type=MESH,
        )

    def pick(made, row, kinds, start):
        total = jnp.zeros((8, row.shape[1]), f32)
        for k in range(kinds):
            total = total + jnp.where(row == float(k + start), made[8 * k : 8 * k + 8], 0.0)
        return total[0:3] + total[3:6]

    per_chunk = z.per_chunk

    def send_back(t):
        table = vel[...].astype(bf16)
        for u in range(z.batch):
            c = t * z.batch + u
            made = dot(table, hot_dst[t, :, u * WIDE : (u + 1) * WIDE])
            done = pick(made, label_dst[c], z.boxes, 1)
            for v in range(per_chunk):
                d = c * per_chunk + v
                back[behind(d)] = done[:, v * z.per_peer : (v + 1) * z.per_peer]
        start = t * z.batch * per_chunk
        loop(
            jnp.maximum(start, 1), start + z.batch * per_chunk, lambda d: back_copy(d).start()
        )

    loop(0, z.chunks // z.batch, send_back)
    returned[me] = back[me]
    loop(1, groups, lambda d: back_copy(d).wait())

    rows = []
    for g in range(groups):
        v1, v2 = pieces(returned[g], 2)
        rows.append(jnp.concatenate([v1, v2, jnp.zeros((2, z.per_peer), f32)], axis=0))
    table = jnp.concatenate(rows, axis=0).astype(bf16)
    for s in range(z.nodes // 512):
        here = slice(s * 512, (s + 1) * 512)
        made = dot(table, hot_src[:, here])
        out[:, here] = pick(made, owner_row[:, here], groups, 0)


def per_device(
    n_age,
    n_box,
    position,
    strength,
    node_box,
    box_order,
    box_center,
    near_list,
    m2l_source,
    m2l_type,
    basis_dir,
    basis_freq,
    basis_phase,
    translation,
):
    z = Sizes(
        n_age, n_box, position.shape[1], box_order.shape[0], basis_phase.shape[0],
        translation.shape[0], m2l_source.shape[1], near_list.shape[1],
    )
    vm = pl.BlockSpec(memory_space=pltpu.VMEM)
    sm = pl.BlockSpec(memory_space=pltpu.SMEM)
    dma = pltpu.SemaphoreType.DMA

    def buf(shape, dtype=f32):
        return pltpu.VMEM(shape, dtype)

    return pl.pallas_call(
        functools.partial(body, z),
        out_shape=jax.ShapeDtypeStruct((3, z.nodes), f32),
        in_specs=[vm, vm, vm, vm, sm, vm, vm, vm, vm, vm, vm, pl.BlockSpec(memory_space=pl.ANY)],
        out_specs=vm,
        scratch_shapes=[
            buf((1, LANES), i32),
            buf((z.groups, 1, LANES), i32),
            buf((8, z.box_total), i32),
            buf((z.groups, 8, z.per_peer)),
            buf((z.groups, 8, z.per_peer)),
            buf((n_age, n_box, z.boxes, z.coef), bf16),
            buf((z.groups, 3, z.per_peer)),
            buf((z.groups, 3, z.per_peer)),
            buf((8, LANES), i32),
            pltpu.SMEM((8, LANES), i32),
            buf(translation.shape, bf16),
            buf((16, z.nodes), bf16),
            buf((z.per_peer, z.nodes), bf16),
            buf((1, z.nodes)),
            buf((16 * z.boxes, z.batch * WIDE), bf16),
            buf((z.chunks // z.batch, z.per_box, z.batch * WIDE), bf16),
            buf((z.chunks, 1, WIDE)),
            buf((16 * z.boxes, z.per_box)),
            buf((z.boxes, 8, z.per_box)),
            buf((z.boxes + 1, 16, z.per_box), bf16),
            buf((z.boxes + 1, z.per_box, 32), bf16),
            buf((z.boxes, 32, z.per_box), bf16),
            buf((z.coef, 48), bf16),
            buf((z.boxes, z.coef, z.per_box), bf16),
            buf((z.boxes, z.coef, z.per_box), bf16),
            buf((z.boxes, z.coef)),
            buf((z.kinds * z.boxes, z.box_total), bf16),
            buf((z.coef // LANES, z.kinds * z.boxes, LANES)),
            buf((z.boxes, 8, z.per_box)),
            buf((8 * z.boxes, z.per_box)),
            dma((2,)),
            dma((2, z.groups - 1)),
            dma((2, z.groups - 1)),
            dma((2, n_age + n_box - 2)),
            dma((2, z.groups - 1)),
        ],
        compiler_params=pltpu.CompilerParams(
            collective_id=0, has_side_effects=True, vmem_limit_bytes=VMEM_LIMIT
        ),
    )(
        position,
        strength,
        node_box.reshape(1, -1),
        box_order.reshape(1, -1),
        box_center,
        near_list.T,
        m2l_source,
        m2l_type,
        basis_dir,
        basis_freq,
        basis_phase.reshape(1, -1),
        translation,
    )


def solution(mesh):
    n_box = mesh.shape["box"]
    n_age = mesh.shape["age"]
    placed = (
        P(None, AXES),
        P(None, AXES),
        P(AXES),
        P(AXES),
        P(None, AXES),
        P(AXES, None),
        P(AXES, None),
        P(AXES, None),
        P(),
        P(),
        P(),
        P(),
    )
    return jax.shard_map(
        functools.partial(per_device, n_age, n_box),
        mesh=mesh,
        in_specs=placed,
        out_specs=P(None, AXES),
        check_vma=False,
    )
```

```python
import functools

import jax
import jax.numpy as jnp
import numpy as np
from jax import lax
from jax.experimental import pallas as pl
from jax.experimental.pallas import tpu as pltpu
from jax.sharding import PartitionSpec as P

AXES = ("age", "box")
MESH = pl.DeviceIdType.MESH
core_square = 0.01
inv_four_pi = 0.07957747154594767
inv_two_pi = 0.15915494309189535
LANES = 128
WIDE = 256
VMEM_LIMIT = 56 * 1024 * 1024
f32, bf16, i32 = jnp.float32, jnp.bfloat16, jnp.int32
NN = (((1,), (0,)), ((), ()))
NT = (((1,), (1,)), ((), ()))


def cos_coefficients(degree):
    nodes = np.cos(np.pi * (np.arange(64) + 0.5) / 64)
    w = 0.125 * (nodes + 1.0)
    fit = np.polynomial.chebyshev.Chebyshev.fit(
        w, np.cos(2 * np.pi * np.sqrt(w)), degree, domain=[0, 0.25]
    )
    return [float(c) for c in fit.convert(kind=np.polynomial.Polynomial).coef]


COS_COEF = cos_coefficients(5)


def cos_turns(turns):
    v = turns - ((turns + 12582912.0) - 12582912.0)
    w = v * v
    acc = jnp.full_like(w, COS_COEF[-1])
    for c in COS_COEF[-2::-1]:
        acc = acc * w + c
    return acc


def dot(a, b, dims=NN):
    return lax.dot_general(a, b, dims, preferred_element_type=f32)


def sublane(rows, n):
    return lax.broadcasted_iota(i32, (rows, n), 0)


def hot(row, rows, start=0):
    steps = (sublane(rows, row.shape[1]) + start).astype(f32).astype(bf16)
    return jnp.where(row.astype(bf16) == steps, jnp.ones((), bf16), jnp.zeros((), bf16))


def pieces(x, count):
    out = []
    for _ in range(count):
        piece = x.astype(bf16).astype(f32)
        out.append(piece)
        x = x - piece
    return out


def two(x):
    return jnp.concatenate(pieces(x, 2), axis=0).astype(bf16)


def cross_parts(a, b):
    return (
        a[1:2] * b[2:3] - a[2:3] * b[1:2],
        a[2:3] * b[0:1] - a[0:1] * b[2:3],
        a[0:1] * b[1:2] - a[1:2] * b[0:1],
    )


def before_table():
    row = sublane(LANES, 2 * LANES)
    col = lax.broadcasted_iota(i32, (LANES, 2 * LANES), 1)
    return jnp.where((row < col) | (col >= LANES), 1.0, 0.0).astype(bf16)


def ranks(hits, before, carry):
    kinds = hits[0].shape[0]
    sums = dot(jnp.concatenate([h.astype(bf16) for h in hits], axis=0), before)
    out = []
    for k, h in enumerate(hits):
        part = sums[k * kinds : (k + 1) * kinds]
        out.append(jnp.sum(h * (part[:, :LANES] + carry), axis=0, keepdims=True))
        carry = carry + part[:, LANES:]
    return out, carry


class Sizes:
    def __init__(self, n_age, n_box, nodes, boxes, coef, kinds, entries, near):
        self.n_age, self.n_box, self.nodes, self.boxes = n_age, n_box, nodes, boxes
        self.coef, self.kinds, self.entries, self.near = coef, kinds, entries, near
        self.groups = n_age * n_box
        self.box_total = self.groups * boxes
        self.digits = self.box_total // 32
        self.slots = 2 * nodes
        self.per_peer = self.slots // self.groups
        self.per_box = self.slots // boxes
        self.per_chunk = WIDE // self.per_peer
        self.chunks = self.slots // WIDE
        self.batch = min(8, self.chunks)


def body(
    z,
    pos, stg, node_box, order, center, near_t, source, kind, direction, freq, phase, translation,
    out,
    order_own, order_all, order_row, pay, recv, blocks, back, returned,
    near_vm, near_sm, trans, fields, hot_src, owner_row, a_buf, hot_dst, label_dst,
    grouped, lanes, parts, src_tab, tgt_tab, freq_t, wave_hi, wave_lo, sums_f, counts, mixed,
    near_vel, vel, local_sem, order_sem, node_sem, block_sem, back_sem,
):
    groups, n_box, n_age = z.groups, z.n_box, z.n_age
    me_age, me_box = lax.axis_index("age"), lax.axis_index("box")
    me = me_age * n_box + me_box
    barrier = pltpu.get_barrier_semaphore()

    def place(other):
        return {"age": other // n_box, "box": lax.rem(other, n_box)}

    def ahead(d):
        return lax.rem(me + d, groups)

    def behind(d):
        return lax.rem(me + groups - d, groups)

    def loop(lo, hi, f, unroll=1):
        def step(i, carry):
            f(i)
            return carry

        lax.fori_loop(lo, hi, step, 0, unroll=unroll)

    loop(
        1, groups,
        lambda d: pl.semaphore_signal(
            barrier, inc=1, device_id=place(ahead(d)), device_id_type=MESH
        ),
    )
    load_translation = pltpu.make_async_copy(translation, trans, local_sem.at[0])
    load_translation.start()
    order_own[...] = jnp.full((1, LANES), -1, i32)
    order_own[:, : z.boxes] = order[...]
    order_all[me] = order_own[...]
    pl.semaphore_wait(barrier, groups - 1)

    def order_copy(d):
        return pltpu.make_async_remote_copy(
            src_ref=order_own,
            dst_ref=order_all.at[me],
            send_sem=order_sem.at[0, d - 1],
            recv_sem=order_sem.at[1, d - 1],
            device_id=place(ahead(d)),
            device_id_type=MESH,
        )

    loop(1, groups, lambda d: order_copy(d).start())

    waves = jnp.concatenate(
        [freq[...], phase[...], jnp.zeros((4, z.coef), f32)], axis=0
    ) * inv_two_pi
    f1, f2, f3 = pieces(waves, 3)
    table = jnp.concatenate(
        [f1, f2, f1, f3, f2, f1, jnp.zeros((LANES - 48, z.coef), f32)], axis=0
    )
    freq_t[...] = table.T[:, :48].astype(bf16)
    before = before_table()

    loop(1, groups, lambda d: order_copy(d).wait())

    m = LANES // z.boxes
    lane8 = lax.broadcasted_iota(i32, (8, LANES), 1)
    for t in range(z.box_total // LANES):
        tile = jnp.broadcast_to(order_all[t * m], (8, LANES))
        for u in range(1, m):
            shifted = pltpu.roll(
                jnp.broadcast_to(order_all[t * m + u], (8, LANES)), u * z.boxes, 1
            )
            tile = jnp.where(lane8 >= u * z.boxes, shifted, tile)
        order_row[:, t * LANES : (t + 1) * LANES] = tile
    ids = order_row[0:1, :]
    at = lax.broadcasted_iota(i32, (1, z.box_total), 1)
    high_hot = sublane(z.digits, z.box_total) == (ids >> 5)
    owner_of = (at // z.boxes).astype(f32)
    label_of = lax.rem(at, z.boxes).astype(f32)
    finder = dot(
        jnp.concatenate(
            [jnp.where(high_hot, owner_of, 0.0), jnp.where(high_hot, label_of, 0.0)], axis=0
        ).astype(bf16),
        hot((ids & 31).astype(f32), 32),
        NT,
    ).astype(bf16)

    def find(box_ids):
        got = dot(finder, hot((box_ids & 31).astype(f32), 32))
        mine = sublane(z.digits, box_ids.shape[1]) == (box_ids >> 5)
        who = jnp.sum(jnp.where(mine, got[: z.digits], 0.0), axis=0, keepdims=True)
        label = jnp.sum(jnp.where(mine, got[z.digits :], 0.0), axis=0, keepdims=True)
        return who, label

    step_nodes = min(1024, z.nodes)
    for s in range(z.nodes // step_nodes):
        here = slice(s * step_nodes, (s + 1) * step_nodes)
        who, label = find(node_box[:, here])
        owner_row[:, here] = who
        fields[:, here] = two(
            jnp.concatenate(
                [pos[:, here], stg[:, here], label + 1.0, jnp.zeros_like(label)], axis=0
            )
        )

    hits = []
    for k in range(z.nodes // LANES):
        row = owner_row[:, k * LANES : (k + 1) * LANES]
        hits.append(jnp.where(sublane(groups, LANES).astype(f32) == row, 1.0, 0.0))
    rank, _ = ranks(hits, before, jnp.zeros((groups, LANES), f32))
    hot_src[...] = hot(jnp.concatenate(rank, axis=1), z.per_peer)

    near_ids = near_t[...]
    for v in range(z.near):
        row = near_ids[v : v + 1]
        _, label = find(row)
        near_vm[v : v + 1, : z.boxes] = jnp.where(row >= 0, label.astype(i32), z.boxes)
    near_copy = pltpu.make_async_copy(near_vm, near_sm, local_sem.at[1])
    near_copy.start()

    def node_copy(d):
        return pltpu.make_async_remote_copy(
            src_ref=pay.at[ahead(d), pl.ds(0, 7)],
            dst_ref=recv.at[me, pl.ds(0, 7)],
            send_sem=node_sem.at[0, d - 1],
            recv_sem=node_sem.at[1, d - 1],
            device_id=place(ahead(d)),
            device_id_type=MESH,
        )

    per_step = min(8, groups)

    def make_payload(k):
        owners = owner_row[...].astype(bf16)
        f = fields[...]
        rows = []
        for u in range(per_step):
            g = ahead(1 + k * per_step + u)
            g16 = jnp.full((1, LANES), g, i32).astype(f32).astype(bf16)[:, :1]
            rows.append(jnp.where(owners == g16, f, jnp.zeros((), bf16)))
        made = dot(jnp.concatenate(rows, axis=0), hot_src[...], NT)
        for u in range(per_step):
            d = 1 + k * per_step + u
            pay[ahead(d)] = made[16 * u : 16 * u + 8] + made[16 * u + 8 : 16 * u + 16]
        start = 1 + k * per_step
        loop(start, jnp.minimum(start + per_step, groups), lambda d: node_copy(d).start())

    loop(0, groups // per_step, make_payload)
    recv[me] = pay[me]

    square = jnp.concatenate(
        [source[...], jnp.zeros((z.boxes, LANES - z.entries), i32)], axis=1
    ).astype(f32)
    square = jnp.concatenate([square, jnp.zeros((LANES - z.boxes, LANES), f32)], axis=0)
    source_t = square.T[: z.entries].astype(i32)
    for j in range(z.boxes):
        from_box = jnp.where(source_t[:, j : j + 1] == ids, 1.0, 0.0).astype(bf16)
        of_kind = jnp.where(
            kind[j : j + 1, :] == sublane(z.kinds, z.entries), 1.0, 0.0
        ).astype(bf16)
        counts[z.kinds * j : z.kinds * (j + 1), :] = dot(of_kind, from_box).astype(bf16)

    def load_chunk(ref, c):
        parts_ = [ref[behind(c * z.per_chunk + v)] for v in range(z.per_chunk)]
        return parts_[0] if z.per_chunk == 1 else jnp.concatenate(parts_, axis=1)

    grouped[...] = jnp.zeros_like(grouped)

    def group_batch(t, carry):
        def arrive(d, c):
            @pl.when(d > 0)
            def _():
                node_copy(d).wait()

            return c

        first = t * z.batch * z.per_chunk
        lax.fori_loop(first, first + z.batch * z.per_chunk, arrive, 0)
        labels, hits, tables = [], [], []
        for u in range(z.batch):
            blk = load_chunk(recv, t * z.batch + u)
            label = blk[6:7]
            label_dst[t * z.batch + u] = label
            labels.append(label)
            tables.append(two(jnp.where(sublane(8, WIDE) < 7, blk, 0.0)))
            for h in range(WIDE // LANES):
                part = label[:, h * LANES : (h + 1) * LANES]
                hits.append(
                    jnp.where((sublane(z.boxes, LANES) + 1).astype(f32) == part, 1.0, 0.0)
                )
        rank, carry = ranks(hits, before_table(), carry)
        per = WIDE // LANES
        for u in range(z.batch):
            row = jnp.concatenate(rank[u * per : (u + 1) * per], axis=1)
            row = jnp.where(labels[u] > 0.0, row, -1.0)
            cols = slice(u * WIDE, (u + 1) * WIDE)
            hot_dst[t, :, cols] = hot(row, z.per_box)
            label16 = labels[u].astype(bf16)
            for b in range(z.boxes):
                a_buf[16 * b : 16 * b + 16, cols] = jnp.where(
                    label16 == jnp.full((), b + 1, bf16), tables[u], jnp.zeros((), bf16)
                )
        grouped[...] += dot(a_buf[...], hot_dst[t], NT)
        return carry

    lax.fori_loop(0, z.chunks // z.batch, group_batch, jnp.zeros((z.boxes, LANES), f32))

    def box_waves(b):
        got = grouped[pl.ds(pl.multiple_of(16 * b, 16), 16), :]
        lan = got[0:8] + got[8:16]
        lanes[b] = lan
        p, s = lan[0:3], lan[3:6]
        n = z.per_box
        zero = jnp.zeros((1, n), f32)
        one = jnp.ones((1, n), f32)
        part = two(jnp.concatenate([s, zero, *cross_parts(s, p), zero], axis=0))
        parts[b] = part
        p1, p2 = got[0:3], got[8:11]
        square = p[0:1] * p[0:1] + p[1:2] * p[1:2] + p[2:3] * p[2:3]
        pad = jnp.zeros((14, n), f32)
        tgt_tab[b] = jnp.concatenate(
            [p1, p1, p2, p2, one, one, one, *pieces(square + core_square, 3), pad], axis=0
        ).astype(bf16)
        src = jnp.concatenate(
            [-2.0 * p1, -2.0 * p2, -2.0 * p1, -2.0 * p2, *pieces(square, 3), one, one, one,
             jnp.zeros((LANES - 18, n), f32)],
            axis=0,
        )
        src_tab[b] = src.T[:, :32].astype(bf16)
        o1, o2, o3 = pieces(
            jnp.concatenate(
                [p[0:1] - center[0, b], p[1:2] - center[1, b], p[2:3] - center[2, b], one,
                 jnp.zeros((4, n), f32)],
                axis=0,
            ),
            3,
        )
        stacked = jnp.concatenate([o3, o2, o2, o1, o1, o1], axis=0).astype(bf16)
        turns = dot(freq_t[...], stacked)
        rows = 32
        highs, lows = [], []
        for c in range(z.coef // rows):
            wave = cos_turns(turns[c * rows : (c + 1) * rows])
            high = wave.astype(bf16)
            highs.append(high)
            lows.append((wave - high.astype(f32)).astype(bf16))
        high = jnp.concatenate(highs, axis=0)
        low = jnp.concatenate(lows, axis=0)
        wave_hi[b] = high
        wave_lo[b] = low
        sums = dot(part, high, NT) + dot(part, low, NT)
        sums = sums[0:8] + sums[8:16]
        sums_f[pl.ds(b, 1), :] = (
            direction[0:1, :] * sums[0:1]
            + direction[1:2, :] * sums[1:2]
            + direction[2:3, :] * sums[2:3]
        )

    loop(0, z.boxes, box_waves, 4)
    parts[z.boxes] = jnp.zeros_like(parts[z.boxes])
    lane32 = lax.broadcasted_iota(i32, (z.per_box, 32), 1)
    src_tab[z.boxes] = jnp.where((lane32 >= 15) & (lane32 < 18), 1.0, 0.0).astype(bf16)
    near_copy.wait()

    blocks[me_age, me_box] = sums_f[...].astype(bf16)

    def along_box(d):
        return pltpu.make_async_remote_copy(
            src_ref=blocks.at[me_age, me_box],
            dst_ref=blocks.at[me_age, me_box],
            send_sem=block_sem.at[0, d - 1],
            recv_sem=block_sem.at[1, d - 1],
            device_id={"age": me_age, "box": lax.rem(me_box + d, n_box)},
            device_id_type=MESH,
        )

    def along_age(d):
        return pltpu.make_async_remote_copy(
            src_ref=blocks.at[me_age],
            dst_ref=blocks.at[me_age],
            send_sem=block_sem.at[0, n_box - 2 + d],
            recv_sem=block_sem.at[1, n_box - 2 + d],
            device_id={"age": lax.rem(me_age + d, n_age), "box": me_box},
            device_id_type=MESH,
        )

    def near_box(b):
        sums = jnp.zeros((16, z.per_box), f32)
        target = tgt_tab[b]
        picks = [jnp.clip(near_sm[v, b], 0, z.boxes) for v in range(z.near)]
        for at in range(0, z.near, 4):
            some = picks[at : at + 4]
            factors = []
            for j in some:
                r = lax.rsqrt(dot(src_tab[j], target))
                factors.append((r * r * r).astype(bf16))
            sums = sums + dot(
                jnp.concatenate([parts[j] for j in some], axis=1),
                jnp.concatenate(factors, axis=0),
            )
        sums = sums[0:8] + sums[8:16]
        at_b = lanes[b]
        pad = jnp.zeros((5, z.per_box), f32)
        near = jnp.concatenate([*cross_parts(sums[0:3], at_b[0:3]), pad], axis=0)
        near_vel[b] = (near - jnp.concatenate([sums[4:7], pad], axis=0)) * inv_four_pi

    first = z.boxes // 4
    loop(1, n_box, lambda d: along_box(d).start())
    loop(0, first, near_box, 4)
    loop(1, n_box, lambda d: along_box(d).wait())
    loop(1, n_age, lambda d: along_age(d).start())
    loop(first, z.boxes, near_box, 4)
    loop(1, n_age, lambda d: along_age(d).wait())
    load_translation.wait()

    every = dot(counts[...], blocks[...].reshape(z.box_total, z.coef))
    for h in range(z.coef // LANES):
        mixed[h] = every[:, h * LANES : (h + 1) * LANES]
    expansion = jnp.zeros((z.boxes, z.coef), f32)
    for t in range(z.kinds):
        rows = [mixed[h, pl.ds(t, z.boxes, stride=z.kinds), :] for h in range(z.coef // LANES)]
        expansion = expansion + dot(jnp.concatenate(rows, axis=1).astype(bf16), trans[t], NT)
    sums_f[...] = expansion

    def far_box(b):
        row = sums_f[pl.ds(b, 1), :]
        table = two(
            jnp.concatenate([direction[...] * row, jnp.zeros((5, z.coef), f32)], axis=0)
        )
        far = dot(table, wave_hi[b]) + dot(table, wave_lo[b])
        total = near_vel[b] + far[0:8] + far[8:16]
        v1, v2 = pieces(total[0:3], 2)
        vel[pl.ds(pl.multiple_of(8 * b, 8), 8), :] = jnp.concatenate(
            [v1, v2, jnp.zeros((2, z.per_box), f32)], axis=0
        )

    loop(0, z.boxes, far_box, 8)

    def back_copy(d):
        return pltpu.make_async_remote_copy(
            src_ref=back.at[behind(d)],
            dst_ref=returned.at[me],
            send_sem=back_sem.at[0, d - 1],
            recv_sem=back_sem.at[1, d - 1],
            device_id=place(behind(d)),
            device_id_type=MESH,
        )

    def pick(made, row, kinds, start):
        total = made[0:8]
        for k in range(1, kinds):
            total = jnp.where(row == float(k + start), made[8 * k : 8 * k + 8], total)
        total = jnp.where(row >= float(start), total, 0.0)
        return total[0:3] + total[3:6]

    per_chunk = z.per_chunk

    def send_back(t):
        table = vel[...].astype(bf16)
        for u in range(z.batch):
            c = t * z.batch + u
            made = dot(table, hot_dst[t, :, u * WIDE : (u + 1) * WIDE])
            done = pick(made, label_dst[c], z.boxes, 1)
            for v in range(per_chunk):
                d = c * per_chunk + v
                back[behind(d)] = done[:, v * z.per_peer : (v + 1) * z.per_peer]
        start = t * z.batch * per_chunk
        loop(
            jnp.maximum(start, 1), start + z.batch * per_chunk, lambda d: back_copy(d).start()
        )

    loop(0, z.chunks // z.batch, send_back)
    returned[me] = back[me]
    loop(1, groups, lambda d: back_copy(d).wait())

    rows = []
    for g in range(groups):
        v1, v2 = pieces(returned[g], 2)
        rows.append(jnp.concatenate([v1, v2, jnp.zeros((2, z.per_peer), f32)], axis=0))
    table = jnp.concatenate(rows, axis=0).astype(bf16)
    for s in range(z.nodes // 512):
        here = slice(s * 512, (s + 1) * 512)
        made = dot(table, hot_src[:, here])
        out[:, here] = pick(made, owner_row[:, here], groups, 0)


def per_device(
    n_age,
    n_box,
    position,
    strength,
    node_box,
    box_order,
    box_center,
    near_list,
    m2l_source,
    m2l_type,
    basis_dir,
    basis_freq,
    basis_phase,
    translation,
):
    z = Sizes(
        n_age, n_box, position.shape[1], box_order.shape[0], basis_phase.shape[0],
        translation.shape[0], m2l_source.shape[1], near_list.shape[1],
    )
    vm = pl.BlockSpec(memory_space=pltpu.VMEM)
    sm = pl.BlockSpec(memory_space=pltpu.SMEM)
    dma = pltpu.SemaphoreType.DMA

    def buf(shape, dtype=f32):
        return pltpu.VMEM(shape, dtype)

    return pl.pallas_call(
        functools.partial(body, z),
        out_shape=jax.ShapeDtypeStruct((3, z.nodes), f32),
        in_specs=[vm, vm, vm, vm, sm, vm, vm, vm, vm, vm, vm, pl.BlockSpec(memory_space=pl.ANY)],
        out_specs=vm,
        scratch_shapes=[
            buf((1, LANES), i32),
            buf((z.groups, 1, LANES), i32),
            buf((8, z.box_total), i32),
            buf((z.groups, 8, z.per_peer)),
            buf((z.groups, 8, z.per_peer)),
            buf((n_age, n_box, z.boxes, z.coef), bf16),
            buf((z.groups, 3, z.per_peer)),
            buf((z.groups, 3, z.per_peer)),
            buf((8, LANES), i32),
            pltpu.SMEM((8, LANES), i32),
            buf(translation.shape, bf16),
            buf((16, z.nodes), bf16),
            buf((z.per_peer, z.nodes), bf16),
            buf((1, z.nodes)),
            buf((16 * z.boxes, z.batch * WIDE), bf16),
            buf((z.chunks // z.batch, z.per_box, z.batch * WIDE), bf16),
            buf((z.chunks, 1, WIDE)),
            buf((16 * z.boxes, z.per_box)),
            buf((z.boxes, 8, z.per_box)),
            buf((z.boxes + 1, 16, z.per_box), bf16),
            buf((z.boxes + 1, z.per_box, 32), bf16),
            buf((z.boxes, 32, z.per_box), bf16),
            buf((z.coef, 48), bf16),
            buf((z.boxes, z.coef, z.per_box), bf16),
            buf((z.boxes, z.coef, z.per_box), bf16),
            buf((z.boxes, z.coef)),
            buf((z.kinds * z.boxes, z.box_total), bf16),
            buf((z.coef // LANES, z.kinds * z.boxes, LANES)),
            buf((z.boxes, 8, z.per_box)),
            buf((8 * z.boxes, z.per_box)),
            dma((2,)),
            dma((2, z.groups - 1)),
            dma((2, z.groups - 1)),
            dma((2, n_age + n_box - 2)),
            dma((2, z.groups - 1)),
        ],
        compiler_params=pltpu.CompilerParams(
            collective_id=0, has_side_effects=True, vmem_limit_bytes=VMEM_LIMIT
        ),
    )(
        position,
        strength,
        node_box.reshape(1, -1),
        box_order.reshape(1, -1),
        box_center,
        near_list.T,
        m2l_source,
        m2l_type,
        basis_dir,
        basis_freq,
        basis_phase.reshape(1, -1),
        translation,
    )


def solution(mesh):
    n_box = mesh.shape["box"]
    n_age = mesh.shape["age"]
    placed = (
        P(None, AXES),
        P(None, AXES),
        P(AXES),
        P(AXES),
        P(None, AXES),
        P(AXES, None),
        P(AXES, None),
        P(AXES, None),
        P(),
        P(),
        P(),
        P(),
    )
    return jax.shard_map(
        functools.partial(per_device, n_age, n_box),
        mesh=mesh,
        in_specs=placed,
        out_specs=P(None, AXES),
        check_vma=False,
    )
```

```python
import functools

import jax
import jax.numpy as jnp
import numpy as np
from jax import lax
from jax.experimental import pallas as pl
from jax.experimental.pallas import tpu as pltpu
from jax.sharding import PartitionSpec as P

AXES = ("age", "box")
MESH = pl.DeviceIdType.MESH
core_square = 0.01
inv_four_pi = 0.07957747154594767
inv_two_pi = 0.15915494309189535
LANES = 128
WIDE = 256
VMEM_LIMIT = 56 * 1024 * 1024
f32, bf16, i32 = jnp.float32, jnp.bfloat16, jnp.int32
NN = (((1,), (0,)), ((), ()))
NT = (((1,), (1,)), ((), ()))


def cos_coefficients(degree):
    nodes = np.cos(np.pi * (np.arange(64) + 0.5) / 64)
    w = 0.125 * (nodes + 1.0)
    fit = np.polynomial.chebyshev.Chebyshev.fit(
        w, np.cos(2 * np.pi * np.sqrt(w)), degree, domain=[0, 0.25]
    )
    return [float(c) for c in fit.convert(kind=np.polynomial.Polynomial).coef]


COS_COEF = cos_coefficients(5)


def cos_turns(turns):
    v = turns - ((turns + 12582912.0) - 12582912.0)
    w = v * v
    acc = jnp.full_like(w, COS_COEF[-1])
    for c in COS_COEF[-2::-1]:
        acc = acc * w + c
    return acc


def dot(a, b, dims=NN):
    return lax.dot_general(a, b, dims, preferred_element_type=f32)


def sublane(rows, n):
    return lax.broadcasted_iota(i32, (rows, n), 0)


def hot(row, rows, start=0):
    steps = (sublane(rows, row.shape[1]) + start).astype(f32).astype(bf16)
    return jnp.where(row.astype(bf16) == steps, jnp.ones((), bf16), jnp.zeros((), bf16))


def pieces(x, count):
    out = []
    for _ in range(count):
        piece = x.astype(bf16).astype(f32)
        out.append(piece)
        x = x - piece
    return out


def two(x):
    return jnp.concatenate(pieces(x, 2), axis=0).astype(bf16)


def cross_parts(a, b):
    return (
        a[1:2] * b[2:3] - a[2:3] * b[1:2],
        a[2:3] * b[0:1] - a[0:1] * b[2:3],
        a[0:1] * b[1:2] - a[1:2] * b[0:1],
    )


def before_table():
    row = sublane(LANES, 2 * LANES)
    col = lax.broadcasted_iota(i32, (LANES, 2 * LANES), 1)
    return jnp.where((row < col) | (col >= LANES), 1.0, 0.0).astype(bf16)


def ranks(hits, before, carry):
    kinds = hits[0].shape[0]
    sums = dot(jnp.concatenate([h.astype(bf16) for h in hits], axis=0), before)
    out = []
    for k, h in enumerate(hits):
        part = sums[k * kinds : (k + 1) * kinds]
        out.append(jnp.sum(h * (part[:, :LANES] + carry), axis=0, keepdims=True))
        carry = carry + part[:, LANES:]
    return out, carry


class Sizes:
    def __init__(self, n_age, n_box, nodes, boxes, coef, kinds, entries, near):
        self.n_age, self.n_box, self.nodes, self.boxes = n_age, n_box, nodes, boxes
        self.coef, self.kinds, self.entries, self.near = coef, kinds, entries, near
        self.groups = n_age * n_box
        self.box_total = self.groups * boxes
        self.digits = self.box_total // 32
        self.slots = 2 * nodes
        self.per_peer = self.slots // self.groups
        self.per_box = self.slots // boxes
        self.per_chunk = WIDE // self.per_peer
        self.chunks = self.slots // WIDE
        self.batch = min(8, self.chunks)


def body(
    z,
    pos, stg, node_box, order, center, near_t, source, kind, direction, freq, phase, translation,
    out,
    order_own, order_all, order_row, pay, recv, blocks, back, returned,
    near_vm, near_sm, trans, fields, hot_src, owner_row, a_buf, hot_dst, label_dst,
    grouped, lanes, parts, src_tab, tgt_tab, freq_t, wave_hi, wave_lo, sums_f, counts, mixed,
    near_vel, vel, local_sem, order_sem, node_sem, block_sem, back_sem,
):
    groups, n_box, n_age = z.groups, z.n_box, z.n_age
    me_age, me_box = lax.axis_index("age"), lax.axis_index("box")
    me = me_age * n_box + me_box
    barrier = pltpu.get_barrier_semaphore()

    def place(other):
        return {"age": other // n_box, "box": lax.rem(other, n_box)}

    def ahead(d):
        return lax.rem(me + d, groups)

    def behind(d):
        return lax.rem(me + groups - d, groups)

    def loop(lo, hi, f, unroll=1):
        def step(i, carry):
            f(i)
            return carry

        lax.fori_loop(lo, hi, step, 0, unroll=unroll)

    loop(
        1, groups,
        lambda d: pl.semaphore_signal(
            barrier, inc=1, device_id=place(ahead(d)), device_id_type=MESH
        ),
    )
    load_translation = pltpu.make_async_copy(translation, trans, local_sem.at[0])
    load_translation.start()
    order_own[...] = jnp.full((1, LANES), -1, i32)
    order_own[:, : z.boxes] = order[...]
    order_all[me] = order_own[...]
    pl.semaphore_wait(barrier, groups - 1)

    def order_copy(d):
        return pltpu.make_async_remote_copy(
            src_ref=order_own,
            dst_ref=order_all.at[me],
            send_sem=order_sem.at[0, d - 1],
            recv_sem=order_sem.at[1, d - 1],
            device_id=place(ahead(d)),
            device_id_type=MESH,
        )

    loop(1, groups, lambda d: order_copy(d).start())

    waves = jnp.concatenate(
        [freq[...], phase[...], jnp.zeros((4, z.coef), f32)], axis=0
    ) * inv_two_pi
    f1, f2, f3 = pieces(waves, 3)
    table = jnp.concatenate(
        [f1, f2, f1, f3, f2, f1, jnp.zeros((LANES - 48, z.coef), f32)], axis=0
    )
    freq_t[...] = table.T[:, :48].astype(bf16)
    before = before_table()

    loop(1, groups, lambda d: order_copy(d).wait())

    m = LANES // z.boxes
    lane8 = lax.broadcasted_iota(i32, (8, LANES), 1)
    for t in range(z.box_total // LANES):
        tile = jnp.broadcast_to(order_all[t * m], (8, LANES))
        for u in range(1, m):
            shifted = pltpu.roll(
                jnp.broadcast_to(order_all[t * m + u], (8, LANES)), u * z.boxes, 1
            )
            tile = jnp.where(lane8 >= u * z.boxes, shifted, tile)
        order_row[:, t * LANES : (t + 1) * LANES] = tile
    ids = order_row[0:1, :]
    at = lax.broadcasted_iota(i32, (1, z.box_total), 1)
    high_hot = sublane(z.digits, z.box_total) == (ids >> 5)
    owner_of = (at // z.boxes).astype(f32)
    label_of = lax.rem(at, z.boxes).astype(f32)
    finder = dot(
        jnp.concatenate(
            [jnp.where(high_hot, owner_of, 0.0), jnp.where(high_hot, label_of, 0.0)], axis=0
        ).astype(bf16),
        hot((ids & 31).astype(f32), 32),
        NT,
    ).astype(bf16)

    def find(box_ids):
        got = dot(finder, hot((box_ids & 31).astype(f32), 32))
        mine = sublane(z.digits, box_ids.shape[1]) == (box_ids >> 5)
        who = jnp.sum(jnp.where(mine, got[: z.digits], 0.0), axis=0, keepdims=True)
        label = jnp.sum(jnp.where(mine, got[z.digits :], 0.0), axis=0, keepdims=True)
        return who, label

    step_nodes = min(1024, z.nodes)
    for s in range(z.nodes // step_nodes):
        here = slice(s * step_nodes, (s + 1) * step_nodes)
        who, label = find(node_box[:, here])
        owner_row[:, here] = who
        fields[:, here] = two(
            jnp.concatenate(
                [pos[:, here], stg[:, here], label + 1.0, jnp.zeros_like(label)], axis=0
            )
        )

    hits = []
    for k in range(z.nodes // LANES):
        row = owner_row[:, k * LANES : (k + 1) * LANES]
        hits.append(jnp.where(sublane(groups, LANES).astype(f32) == row, 1.0, 0.0))
    rank, _ = ranks(hits, before, jnp.zeros((groups, LANES), f32))
    hot_src[...] = hot(jnp.concatenate(rank, axis=1), z.per_peer)

    near_ids = near_t[...]
    for v in range(z.near):
        row = near_ids[v : v + 1]
        _, label = find(row)
        near_vm[v : v + 1, : z.boxes] = jnp.where(row >= 0, label.astype(i32), z.boxes)
    near_copy = pltpu.make_async_copy(near_vm, near_sm, local_sem.at[1])
    near_copy.start()

    def node_copy(d):
        return pltpu.make_async_remote_copy(
            src_ref=pay.at[ahead(d), pl.ds(0, 7)],
            dst_ref=recv.at[me, pl.ds(0, 7)],
            send_sem=node_sem.at[0, d - 1],
            recv_sem=node_sem.at[1, d - 1],
            device_id=place(ahead(d)),
            device_id_type=MESH,
        )

    per_step = min(8, groups)

    def make_payload(k):
        owners = owner_row[...].astype(bf16)
        f = fields[...]
        rows = []
        for u in range(per_step):
            g = ahead(1 + k * per_step + u)
            g16 = jnp.full((1, LANES), g, i32).astype(f32).astype(bf16)[:, :1]
            rows.append(jnp.where(owners == g16, f, jnp.zeros((), bf16)))
        made = dot(jnp.concatenate(rows, axis=0), hot_src[...], NT)
        for u in range(per_step):
            d = 1 + k * per_step + u
            pay[ahead(d)] = made[16 * u : 16 * u + 8] + made[16 * u + 8 : 16 * u + 16]
        start = 1 + k * per_step
        loop(start, jnp.minimum(start + per_step, groups), lambda d: node_copy(d).start())

    loop(0, groups // per_step, make_payload)
    recv[me] = pay[me]

    square = jnp.concatenate(
        [source[...], jnp.zeros((z.boxes, LANES - z.entries), i32)], axis=1
    ).astype(f32)
    square = jnp.concatenate([square, jnp.zeros((LANES - z.boxes, LANES), f32)], axis=0)
    source_t = square.T[: z.entries].astype(i32)
    for j in range(z.boxes):
        from_box = jnp.where(source_t[:, j : j + 1] == ids, 1.0, 0.0).astype(bf16)
        of_kind = jnp.where(
            kind[j : j + 1, :] == sublane(z.kinds, z.entries), 1.0, 0.0
        ).astype(bf16)
        counts[z.kinds * j : z.kinds * (j + 1), :] = dot(of_kind, from_box).astype(bf16)

    def load_chunk(ref, c):
        parts_ = [ref[behind(c * z.per_chunk + v)] for v in range(z.per_chunk)]
        return parts_[0] if z.per_chunk == 1 else jnp.concatenate(parts_, axis=1)

    grouped[...] = jnp.zeros_like(grouped)

    def group_batch(t, carry):
        def arrive(d, c):
            @pl.when(d > 0)
            def _():
                node_copy(d).wait()

            return c

        first = t * z.batch * z.per_chunk
        lax.fori_loop(first, first + z.batch * z.per_chunk, arrive, 0)
        labels, hits, tables = [], [], []
        for u in range(z.batch):
            blk = load_chunk(recv, t * z.batch + u)
            label = blk[6:7]
            label_dst[t * z.batch + u] = label
            labels.append(label)
            tables.append(two(jnp.where(sublane(8, WIDE) < 7, blk, 0.0)))
            for h in range(WIDE // LANES):
                part = label[:, h * LANES : (h + 1) * LANES]
                hits.append(
                    jnp.where((sublane(z.boxes, LANES) + 1).astype(f32) == part, 1.0, 0.0)
                )
        rank, carry = ranks(hits, before_table(), carry)
        per = WIDE // LANES
        for u in range(z.batch):
            row = jnp.concatenate(rank[u * per : (u + 1) * per], axis=1)
            row = jnp.where(labels[u] > 0.0, row, -1.0)
            cols = slice(u * WIDE, (u + 1) * WIDE)
            hot_dst[t, :, cols] = hot(row, z.per_box)
            label16 = labels[u].astype(bf16)
            for b in range(z.boxes):
                a_buf[16 * b : 16 * b + 16, cols] = jnp.where(
                    label16 == jnp.full((), b + 1, bf16), tables[u], jnp.zeros((), bf16)
                )
        grouped[...] += dot(a_buf[...], hot_dst[t], NT)
        return carry

    lax.fori_loop(0, z.chunks // z.batch, group_batch, jnp.zeros((z.boxes, LANES), f32))

    def box_waves(b):
        got = grouped[pl.ds(pl.multiple_of(16 * b, 16), 16), :]
        lan = got[0:8] + got[8:16]
        lanes[b] = lan
        p, s = lan[0:3], lan[3:6]
        n = z.per_box
        zero = jnp.zeros((1, n), f32)
        one = jnp.ones((1, n), f32)
        part = two(jnp.concatenate([s, zero, *cross_parts(s, p), zero], axis=0))
        parts[b] = part
        p1, p2 = got[0:3], got[8:11]
        square = p[0:1] * p[0:1] + p[1:2] * p[1:2] + p[2:3] * p[2:3]
        pad = jnp.zeros((14, n), f32)
        tgt_tab[b] = jnp.concatenate(
            [p1, p1, p2, p2, one, one, one, *pieces(square + core_square, 3), pad], axis=0
        ).astype(bf16)
        src = jnp.concatenate(
            [-2.0 * p1, -2.0 * p2, -2.0 * p1, -2.0 * p2, *pieces(square, 3), one, one, one,
             jnp.zeros((LANES - 18, n), f32)],
            axis=0,
        )
        src_tab[b] = src.T[:, :32].astype(bf16)
        o1, o2, o3 = pieces(
            jnp.concatenate(
                [p[0:1] - center[0, b], p[1:2] - center[1, b], p[2:3] - center[2, b], one,
                 jnp.zeros((4, n), f32)],
                axis=0,
            ),
            3,
        )
        stacked = jnp.concatenate([o3, o2, o2, o1, o1, o1], axis=0).astype(bf16)
        turns = dot(freq_t[...], stacked)
        rows = 32
        highs, lows = [], []
        for c in range(z.coef // rows):
            wave = cos_turns(turns[c * rows : (c + 1) * rows])
            high = wave.astype(bf16)
            highs.append(high)
            lows.append((wave - high.astype(f32)).astype(bf16))
        high = jnp.concatenate(highs, axis=0)
        low = jnp.concatenate(lows, axis=0)
        wave_hi[b] = high
        wave_lo[b] = low
        sums = dot(part, high, NT) + dot(part, low, NT)
        sums = sums[0:8] + sums[8:16]
        sums_f[pl.ds(b, 1), :] = (
            direction[0:1, :] * sums[0:1]
            + direction[1:2, :] * sums[1:2]
            + direction[2:3, :] * sums[2:3]
        )

    loop(0, z.boxes, box_waves, 4)
    parts[z.boxes] = jnp.zeros_like(parts[z.boxes])
    lane32 = lax.broadcasted_iota(i32, (z.per_box, 32), 1)
    src_tab[z.boxes] = jnp.where((lane32 >= 15) & (lane32 < 18), 1.0, 0.0).astype(bf16)
    near_copy.wait()

    blocks[me_age, me_box] = sums_f[...].astype(bf16)

    def along_box(d):
        return pltpu.make_async_remote_copy(
            src_ref=blocks.at[me_age, me_box],
            dst_ref=blocks.at[me_age, me_box],
            send_sem=block_sem.at[0, d - 1],
            recv_sem=block_sem.at[1, d - 1],
            device_id={"age": me_age, "box": lax.rem(me_box + d, n_box)},
            device_id_type=MESH,
        )

    def along_age(d):
        return pltpu.make_async_remote_copy(
            src_ref=blocks.at[me_age],
            dst_ref=blocks.at[me_age],
            send_sem=block_sem.at[0, n_box - 2 + d],
            recv_sem=block_sem.at[1, n_box - 2 + d],
            device_id={"age": lax.rem(me_age + d, n_age), "box": me_box},
            device_id_type=MESH,
        )

    def near_box(b):
        sums = jnp.zeros((16, z.per_box), f32)
        target = tgt_tab[b]
        picks = [jnp.clip(near_sm[v, b], 0, z.boxes) for v in range(z.near)]
        for at in range(0, z.near, 4):
            some = picks[at : at + 4]
            factors = []
            for j in some:
                r = lax.rsqrt(dot(src_tab[j], target))
                factors.append((r * r * r).astype(bf16))
            sums = sums + dot(
                jnp.concatenate([parts[j] for j in some], axis=1),
                jnp.concatenate(factors, axis=0),
            )
        sums = sums[0:8] + sums[8:16]
        at_b = lanes[b]
        pad = jnp.zeros((5, z.per_box), f32)
        near = jnp.concatenate([*cross_parts(sums[0:3], at_b[0:3]), pad], axis=0)
        near_vel[b] = (near - jnp.concatenate([sums[4:7], pad], axis=0)) * inv_four_pi

    first = 3 * z.boxes // 8
    loop(1, n_box, lambda d: along_box(d).start())
    loop(0, first, near_box, 4)
    loop(1, n_box, lambda d: along_box(d).wait())
    loop(1, n_age, lambda d: along_age(d).start())
    loop(first, z.boxes, near_box, 4)
    loop(1, n_age, lambda d: along_age(d).wait())
    load_translation.wait()

    every = dot(counts[...], blocks[...].reshape(z.box_total, z.coef))
    for h in range(z.coef // LANES):
        mixed[h] = every[:, h * LANES : (h + 1) * LANES]
    expansion = jnp.zeros((z.boxes, z.coef), f32)
    for t in range(z.kinds):
        rows = [mixed[h, pl.ds(t, z.boxes, stride=z.kinds), :] for h in range(z.coef // LANES)]
        expansion = expansion + dot(jnp.concatenate(rows, axis=1).astype(bf16), trans[t], NT)
    sums_f[...] = expansion

    def far_box(b):
        row = sums_f[pl.ds(b, 1), :]
        table = two(
            jnp.concatenate([direction[...] * row, jnp.zeros((5, z.coef), f32)], axis=0)
        )
        far = dot(table, wave_hi[b]) + dot(table, wave_lo[b])
        total = near_vel[b] + far[0:8] + far[8:16]
        vel[b] = total[0:4]

    loop(0, z.boxes, far_box, 16)

    def back_copy(d):
        return pltpu.make_async_remote_copy(
            src_ref=back.at[behind(d)],
            dst_ref=returned.at[me],
            send_sem=back_sem.at[0, d - 1],
            recv_sem=back_sem.at[1, d - 1],
            device_id=place(behind(d)),
            device_id_type=MESH,
        )

    def spread(ref, rows):
        high, low = pieces(ref[...].reshape(rows, ref.shape[2]), 2)
        return high.astype(bf16), low.astype(bf16)

    def pick(made, row, kinds, start):
        half = sublane(8, row.shape[1]) // 4
        even = jnp.where(half == 0, row, row - 1.0)
        total = made[0:8]
        for k in range(2, kinds, 2):
            total = jnp.where(even == float(k + start), made[4 * k : 4 * k + 8], total)
        total = jnp.where(lax.rem((row - start).astype(i32), 2) == half, total, 0.0)
        total = jnp.where(row >= float(start), total, 0.0)
        return total[0:4] + total[4:8]

    per_chunk = z.per_chunk

    def send_back(t):
        high, low = spread(vel, 4 * z.boxes)
        for u in range(z.batch):
            c = t * z.batch + u
            hot_u = hot_dst[t, :, u * WIDE : (u + 1) * WIDE]
            made = dot(high, hot_u) + dot(low, hot_u)
            done = pick(made, label_dst[c], z.boxes, 1)
            for v in range(per_chunk):
                d = c * per_chunk + v
                back[behind(d)] = done[:, v * z.per_peer : (v + 1) * z.per_peer]
        start = t * z.batch * per_chunk
        loop(
            jnp.maximum(start, 1), start + z.batch * per_chunk, lambda d: back_copy(d).start()
        )

    loop(0, z.chunks // z.batch, send_back)
    returned[me] = back[me]
    loop(1, groups, lambda d: back_copy(d).wait())

    high, low = spread(returned, 4 * groups)
    for s in range(z.nodes // 512):
        here = slice(s * 512, (s + 1) * 512)
        made = dot(high, hot_src[:, here]) + dot(low, hot_src[:, here])
        out[:, here] = pick(made, owner_row[:, here], groups, 0)[0:3]


def per_device(
    n_age,
    n_box,
    position,
    strength,
    node_box,
    box_order,
    box_center,
    near_list,
    m2l_source,
    m2l_type,
    basis_dir,
    basis_freq,
    basis_phase,
    translation,
):
    z = Sizes(
        n_age, n_box, position.shape[1], box_order.shape[0], basis_phase.shape[0],
        translation.shape[0], m2l_source.shape[1], near_list.shape[1],
    )
    vm = pl.BlockSpec(memory_space=pltpu.VMEM)
    sm = pl.BlockSpec(memory_space=pltpu.SMEM)
    dma = pltpu.SemaphoreType.DMA

    def buf(shape, dtype=f32):
        return pltpu.VMEM(shape, dtype)

    return pl.pallas_call(
        functools.partial(body, z),
        out_shape=jax.ShapeDtypeStruct((3, z.nodes), f32),
        in_specs=[vm, vm, vm, vm, sm, vm, vm, vm, vm, vm, vm, pl.BlockSpec(memory_space=pl.ANY)],
        out_specs=vm,
        scratch_shapes=[
            buf((1, LANES), i32),
            buf((z.groups, 1, LANES), i32),
            buf((8, z.box_total), i32),
            buf((z.groups, 8, z.per_peer)),
            buf((z.groups, 8, z.per_peer)),
            buf((n_age, n_box, z.boxes, z.coef), bf16),
            buf((z.groups, 4, z.per_peer)),
            buf((z.groups, 4, z.per_peer)),
            buf((8, LANES), i32),
            pltpu.SMEM((8, LANES), i32),
            buf(translation.shape, bf16),
            buf((16, z.nodes), bf16),
            buf((z.per_peer, z.nodes), bf16),
            buf((1, z.nodes)),
            buf((16 * z.boxes, z.batch * WIDE), bf16),
            buf((z.chunks // z.batch, z.per_box, z.batch * WIDE), bf16),
            buf((z.chunks, 1, WIDE)),
            buf((16 * z.boxes, z.per_box)),
            buf((z.boxes, 8, z.per_box)),
            buf((z.boxes + 1, 16, z.per_box), bf16),
            buf((z.boxes + 1, z.per_box, 32), bf16),
            buf((z.boxes, 32, z.per_box), bf16),
            buf((z.coef, 48), bf16),
            buf((z.boxes, z.coef, z.per_box), bf16),
            buf((z.boxes, z.coef, z.per_box), bf16),
            buf((z.boxes, z.coef)),
            buf((z.kinds * z.boxes, z.box_total), bf16),
            buf((z.coef // LANES, z.kinds * z.boxes, LANES)),
            buf((z.boxes, 8, z.per_box)),
            buf((z.boxes, 4, z.per_box)),
            dma((2,)),
            dma((2, z.groups - 1)),
            dma((2, z.groups - 1)),
            dma((2, n_age + n_box - 2)),
            dma((2, z.groups - 1)),
        ],
        compiler_params=pltpu.CompilerParams(
            collective_id=0, has_side_effects=True, vmem_limit_bytes=VMEM_LIMIT
        ),
    )(
        position,
        strength,
        node_box.reshape(1, -1),
        box_order.reshape(1, -1),
        box_center,
        near_list.T,
        m2l_source,
        m2l_type,
        basis_dir,
        basis_freq,
        basis_phase.reshape(1, -1),
        translation,
    )


def solution(mesh):
    n_box = mesh.shape["box"]
    n_age = mesh.shape["age"]
    placed = (
        P(None, AXES),
        P(None, AXES),
        P(AXES),
        P(AXES),
        P(None, AXES),
        P(AXES, None),
        P(AXES, None),
        P(AXES, None),
        P(),
        P(),
        P(),
        P(),
    )
    return jax.shard_map(
        functools.partial(per_device, n_age, n_box),
        mesh=mesh,
        in_specs=placed,
        out_specs=P(None, AXES),
        check_vma=False,
    )
```

```python
import functools

import jax
import jax.numpy as jnp
import numpy as np
from jax import lax
from jax.experimental import pallas as pl
from jax.experimental.pallas import tpu as pltpu
from jax.sharding import PartitionSpec as P

AXES = ("age", "box")
MESH = pl.DeviceIdType.MESH
core_square = 0.01
inv_four_pi = 0.07957747154594767
inv_two_pi = 0.15915494309189535
LANES = 128
WIDE = 256
VMEM_LIMIT = 56 * 1024 * 1024
f32, bf16, i32 = jnp.float32, jnp.bfloat16, jnp.int32
NN = (((1,), (0,)), ((), ()))
NT = (((1,), (1,)), ((), ()))


def cos_coefficients(degree):
    nodes = np.cos(np.pi * (np.arange(64) + 0.5) / 64)
    w = 0.125 * (nodes + 1.0)
    fit = np.polynomial.chebyshev.Chebyshev.fit(
        w, np.cos(2 * np.pi * np.sqrt(w)), degree, domain=[0, 0.25]
    )
    return [float(c) for c in fit.convert(kind=np.polynomial.Polynomial).coef]


COS_COEF = cos_coefficients(5)
COS_TOP = COS_COEF[-1]


def cos_turns(turns):
    v = turns - ((turns + 12582912.0) - 12582912.0)
    w = v * v
    acc = w + COS_COEF[-2] / COS_TOP
    for c in COS_COEF[-3::-1]:
        acc = acc * w + c / COS_TOP
    return acc


def dot(a, b, dims=NN):
    return lax.dot_general(a, b, dims, preferred_element_type=f32)


def sublane(rows, n):
    return lax.broadcasted_iota(i32, (rows, n), 0)


def hot(row, rows, start=0):
    steps = (sublane(rows, row.shape[1]) + start).astype(f32).astype(bf16)
    return jnp.where(row.astype(bf16) == steps, jnp.ones((), bf16), jnp.zeros((), bf16))


def pieces(x, count):
    out = []
    for _ in range(count):
        piece = x.astype(bf16).astype(f32)
        out.append(piece)
        x = x - piece
    return out


def two(x):
    return jnp.concatenate(pieces(x, 2), axis=0).astype(bf16)


def cross_parts(a, b):
    return (
        a[1:2] * b[2:3] - a[2:3] * b[1:2],
        a[2:3] * b[0:1] - a[0:1] * b[2:3],
        a[0:1] * b[1:2] - a[1:2] * b[0:1],
    )


def before_table():
    row = sublane(LANES, 2 * LANES)
    col = lax.broadcasted_iota(i32, (LANES, 2 * LANES), 1)
    return jnp.where((row < col) | (col >= LANES), 1.0, 0.0).astype(bf16)


def ranks(hits, before, carry):
    kinds = hits[0].shape[0]
    sums = dot(jnp.concatenate([h.astype(bf16) for h in hits], axis=0), before)
    out = []
    for k, h in enumerate(hits):
        part = sums[k * kinds : (k + 1) * kinds]
        out.append(jnp.sum(h * (part[:, :LANES] + carry), axis=0, keepdims=True))
        carry = carry + part[:, LANES:]
    return out, carry


class Sizes:
    def __init__(self, n_age, n_box, nodes, boxes, coef, kinds, entries, near):
        self.n_age, self.n_box, self.nodes, self.boxes = n_age, n_box, nodes, boxes
        self.coef, self.kinds, self.entries, self.near = coef, kinds, entries, near
        self.groups = n_age * n_box
        self.box_total = self.groups * boxes
        self.digits = self.box_total // 32
        self.slots = 2 * nodes
        self.per_peer = self.slots // self.groups
        self.per_box = self.slots // boxes
        self.per_chunk = WIDE // self.per_peer
        self.chunks = self.slots // WIDE
        self.batch = min(8, self.chunks)


def body(
    z,
    pos, stg, node_box, order, center, near_t, source, kind, direction, freq, phase, translation,
    out,
    order_own, order_all, order_row, pay, recv, blocks, back, returned,
    near_vm, near_sm, trans, fields, hot_src, owner_row, a_buf, hot_dst, label_dst,
    grouped, lanes, parts, src_tab, tgt_tab, freq_t, wave_hi, wave_lo, sums_f, counts, mixed,
    near_vel, vel, local_sem, order_sem, node_sem, block_sem, back_sem,
):
    groups, n_box, n_age = z.groups, z.n_box, z.n_age
    me_age, me_box = lax.axis_index("age"), lax.axis_index("box")
    me = me_age * n_box + me_box
    barrier = pltpu.get_barrier_semaphore()

    def place(other):
        return {"age": other // n_box, "box": lax.rem(other, n_box)}

    def ahead(d):
        return lax.rem(me + d, groups)

    def behind(d):
        return lax.rem(me + groups - d, groups)

    def loop(lo, hi, f, unroll=1):
        def step(i, carry):
            f(i)
            return carry

        lax.fori_loop(lo, hi, step, 0, unroll=unroll)

    loop(
        1, groups,
        lambda d: pl.semaphore_signal(
            barrier, inc=1, device_id=place(ahead(d)), device_id_type=MESH
        ),
    )
    load_translation = pltpu.make_async_copy(translation, trans, local_sem.at[0])
    load_translation.start()
    order_own[...] = jnp.full((1, LANES), -1, i32)
    order_own[:, : z.boxes] = order[...]
    order_all[me] = order_own[...]
    pl.semaphore_wait(barrier, groups - 1)

    def order_copy(d):
        return pltpu.make_async_remote_copy(
            src_ref=order_own,
            dst_ref=order_all.at[me],
            send_sem=order_sem.at[0, d - 1],
            recv_sem=order_sem.at[1, d - 1],
            device_id=place(ahead(d)),
            device_id_type=MESH,
        )

    loop(1, groups, lambda d: order_copy(d).start())

    waves = jnp.concatenate(
        [freq[...], phase[...], jnp.zeros((4, z.coef), f32)], axis=0
    ) * inv_two_pi
    f1, f2, f3 = pieces(waves, 3)
    table = jnp.concatenate(
        [f1, f2, f1, f3, f2, f1, jnp.zeros((LANES - 48, z.coef), f32)], axis=0
    )
    freq_t[...] = table.T[:, :48].astype(bf16)
    before = before_table()

    loop(1, groups, lambda d: order_copy(d).wait())

    m = LANES // z.boxes
    lane8 = lax.broadcasted_iota(i32, (8, LANES), 1)
    for t in range(z.box_total // LANES):
        tile = jnp.broadcast_to(order_all[t * m], (8, LANES))
        for u in range(1, m):
            shifted = pltpu.roll(
                jnp.broadcast_to(order_all[t * m + u], (8, LANES)), u * z.boxes, 1
            )
            tile = jnp.where(lane8 >= u * z.boxes, shifted, tile)
        order_row[:, t * LANES : (t + 1) * LANES] = tile
    ids = order_row[0:1, :]
    at = lax.broadcasted_iota(i32, (1, z.box_total), 1)
    high_hot = sublane(z.digits, z.box_total) == (ids >> 5)
    owner_of = (at // z.boxes).astype(f32)
    label_of = lax.rem(at, z.boxes).astype(f32)
    finder = dot(
        jnp.concatenate(
            [jnp.where(high_hot, owner_of, 0.0), jnp.where(high_hot, label_of, 0.0)], axis=0
        ).astype(bf16),
        hot((ids & 31).astype(f32), 32),
        NT,
    ).astype(bf16)

    def find(box_ids):
        got = dot(finder, hot((box_ids & 31).astype(f32), 32))
        mine = sublane(z.digits, box_ids.shape[1]) == (box_ids >> 5)
        who = jnp.sum(jnp.where(mine, got[: z.digits], 0.0), axis=0, keepdims=True)
        label = jnp.sum(jnp.where(mine, got[z.digits :], 0.0), axis=0, keepdims=True)
        return who, label

    step_nodes = min(1024, z.nodes)
    for s in range(z.nodes // step_nodes):
        here = slice(s * step_nodes, (s + 1) * step_nodes)
        who, label = find(node_box[:, here])
        owner_row[:, here] = who
        fields[:, here] = two(
            jnp.concatenate(
                [pos[:, here], stg[:, here], label + 1.0, jnp.zeros_like(label)], axis=0
            )
        )

    hits = []
    for k in range(z.nodes // LANES):
        row = owner_row[:, k * LANES : (k + 1) * LANES]
        hits.append(jnp.where(sublane(groups, LANES).astype(f32) == row, 1.0, 0.0))
    rank, _ = ranks(hits, before, jnp.zeros((groups, LANES), f32))
    hot_src[...] = hot(jnp.concatenate(rank, axis=1), z.per_peer)

    near_ids = near_t[...]
    for v in range(z.near):
        row = near_ids[v : v + 1]
        _, label = find(row)
        near_vm[v : v + 1, : z.boxes] = jnp.where(row >= 0, label.astype(i32), z.boxes)
    near_copy = pltpu.make_async_copy(near_vm, near_sm, local_sem.at[1])
    near_copy.start()

    def node_copy(d):
        return pltpu.make_async_remote_copy(
            src_ref=pay.at[ahead(d), pl.ds(0, 7)],
            dst_ref=recv.at[me, pl.ds(0, 7)],
            send_sem=node_sem.at[0, d - 1],
            recv_sem=node_sem.at[1, d - 1],
            device_id=place(ahead(d)),
            device_id_type=MESH,
        )

    per_step = min(8, groups)

    def make_payload(k):
        owners = owner_row[...].astype(bf16)
        f = fields[...]
        rows = []
        for u in range(per_step):
            g = ahead(1 + k * per_step + u)
            g16 = jnp.full((1, LANES), g, i32).astype(f32).astype(bf16)[:, :1]
            rows.append(jnp.where(owners == g16, f, jnp.zeros((), bf16)))
        made = dot(jnp.concatenate(rows, axis=0), hot_src[...], NT)
        for u in range(per_step):
            d = 1 + k * per_step + u
            pay[ahead(d)] = made[16 * u : 16 * u + 8] + made[16 * u + 8 : 16 * u + 16]
        start = 1 + k * per_step
        loop(start, jnp.minimum(start + per_step, groups), lambda d: node_copy(d).start())

    loop(0, groups // per_step, make_payload)
    recv[me] = pay[me]

    square = jnp.concatenate(
        [source[...], jnp.zeros((z.boxes, LANES - z.entries), i32)], axis=1
    ).astype(f32)
    square = jnp.concatenate([square, jnp.zeros((LANES - z.boxes, LANES), f32)], axis=0)
    source_t = square.T[: z.entries].astype(i32)
    for j in range(z.boxes):
        from_box = jnp.where(source_t[:, j : j + 1] == ids, 1.0, 0.0).astype(bf16)
        of_kind = jnp.where(
            kind[j : j + 1, :] == sublane(z.kinds, z.entries), 1.0, 0.0
        ).astype(bf16)
        counts[z.kinds * j : z.kinds * (j + 1), :] = dot(of_kind, from_box).astype(bf16)

    def load_chunk(ref, c):
        parts_ = [ref[behind(c * z.per_chunk + v)] for v in range(z.per_chunk)]
        return parts_[0] if z.per_chunk == 1 else jnp.concatenate(parts_, axis=1)

    grouped[...] = jnp.zeros_like(grouped)

    def group_batch(t, carry):
        def arrive(d, c):
            @pl.when(d > 0)
            def _():
                node_copy(d).wait()

            return c

        first = t * z.batch * z.per_chunk
        lax.fori_loop(first, first + z.batch * z.per_chunk, arrive, 0)
        labels, hits, tables = [], [], []
        for u in range(z.batch):
            blk = load_chunk(recv, t * z.batch + u)
            label = blk[6:7]
            label_dst[t * z.batch + u] = label
            labels.append(label)
            tables.append(two(jnp.where(sublane(8, WIDE) < 7, blk, 0.0)))
            for h in range(WIDE // LANES):
                part = label[:, h * LANES : (h + 1) * LANES]
                hits.append(
                    jnp.where((sublane(z.boxes, LANES) + 1).astype(f32) == part, 1.0, 0.0)
                )
        rank, carry = ranks(hits, before_table(), carry)
        per = WIDE // LANES
        for u in range(z.batch):
            row = jnp.concatenate(rank[u * per : (u + 1) * per], axis=1)
            row = jnp.where(labels[u] > 0.0, row, -1.0)
            cols = slice(u * WIDE, (u + 1) * WIDE)
            hot_dst[t, :, cols] = hot(row, z.per_box)
            label16 = labels[u].astype(bf16)
            for b in range(z.boxes):
                a_buf[16 * b : 16 * b + 16, cols] = jnp.where(
                    label16 == jnp.full((), b + 1, bf16), tables[u], jnp.zeros((), bf16)
                )
        grouped[...] += dot(a_buf[...], hot_dst[t], NT)
        return carry

    lax.fori_loop(0, z.chunks // z.batch, group_batch, jnp.zeros((z.boxes, LANES), f32))

    def box_waves(b):
        got = grouped[pl.ds(pl.multiple_of(16 * b, 16), 16), :]
        lan = got[0:8] + got[8:16]
        lanes[b] = lan
        p, s = lan[0:3], lan[3:6]
        n = z.per_box
        zero = jnp.zeros((1, n), f32)
        one = jnp.ones((1, n), f32)
        part = two(jnp.concatenate([s, zero, *cross_parts(s, p), zero], axis=0))
        parts[b] = part
        p1, p2 = got[0:3], got[8:11]
        square = p[0:1] * p[0:1] + p[1:2] * p[1:2] + p[2:3] * p[2:3]
        pad = jnp.zeros((14, n), f32)
        tgt_tab[b] = jnp.concatenate(
            [p1, p1, p2, p2, one, one, one, *pieces(square + core_square, 3), pad], axis=0
        ).astype(bf16)
        src = jnp.concatenate(
            [-2.0 * p1, -2.0 * p2, -2.0 * p1, -2.0 * p2, *pieces(square, 3), one, one, one,
             jnp.zeros((LANES - 18, n), f32)],
            axis=0,
        )
        src_tab[b] = src.T[:, :32].astype(bf16)
        o1, o2, o3 = pieces(
            jnp.concatenate(
                [p[0:1] - center[0, b], p[1:2] - center[1, b], p[2:3] - center[2, b], one,
                 jnp.zeros((4, n), f32)],
                axis=0,
            ),
            3,
        )
        stacked = jnp.concatenate([o3, o2, o2, o1, o1, o1], axis=0).astype(bf16)
        turns = dot(freq_t[...], stacked)
        rows = 32
        highs, lows = [], []
        for c in range(z.coef // rows):
            wave = cos_turns(turns[c * rows : (c + 1) * rows])
            high = wave.astype(bf16)
            highs.append(high)
            lows.append((wave - high.astype(f32)).astype(bf16))
        high = jnp.concatenate(highs, axis=0)
        low = jnp.concatenate(lows, axis=0)
        wave_hi[b] = high
        wave_lo[b] = low
        sums = dot(part, high, NT) + dot(part, low, NT)
        sums = sums[0:8] + sums[8:16]
        sums_f[pl.ds(b, 1), :] = COS_TOP * (
            direction[0:1, :] * sums[0:1]
            + direction[1:2, :] * sums[1:2]
            + direction[2:3, :] * sums[2:3]
        )

    loop(0, z.boxes, box_waves, 4)
    parts[z.boxes] = jnp.zeros_like(parts[z.boxes])
    lane32 = lax.broadcasted_iota(i32, (z.per_box, 32), 1)
    src_tab[z.boxes] = jnp.where((lane32 >= 15) & (lane32 < 18), 1.0, 0.0).astype(bf16)
    near_copy.wait()

    blocks[me_age, me_box] = sums_f[...].astype(bf16)

    def along_box(d):
        return pltpu.make_async_remote_copy(
            src_ref=blocks.at[me_age, me_box],
            dst_ref=blocks.at[me_age, me_box],
            send_sem=block_sem.at[0, d - 1],
            recv_sem=block_sem.at[1, d - 1],
            device_id={"age": me_age, "box": lax.rem(me_box + d, n_box)},
            device_id_type=MESH,
        )

    def along_age(d):
        return pltpu.make_async_remote_copy(
            src_ref=blocks.at[me_age],
            dst_ref=blocks.at[me_age],
            send_sem=block_sem.at[0, n_box - 2 + d],
            recv_sem=block_sem.at[1, n_box - 2 + d],
            device_id={"age": lax.rem(me_age + d, n_age), "box": me_box},
            device_id_type=MESH,
        )

    def near_box(b):
        sums = jnp.zeros((16, z.per_box), f32)
        target = tgt_tab[b]
        picks = [jnp.clip(near_sm[v, b], 0, z.boxes) for v in range(z.near)]
        for at in range(0, z.near, 4):
            some = picks[at : at + 4]
            factors = []
            for j in some:
                r = lax.rsqrt(dot(src_tab[j], target))
                factors.append((r * r * r).astype(bf16))
            sums = sums + dot(
                jnp.concatenate([parts[j] for j in some], axis=1),
                jnp.concatenate(factors, axis=0),
            )
        sums = sums[0:8] + sums[8:16]
        at_b = lanes[b]
        pad = jnp.zeros((5, z.per_box), f32)
        near = jnp.concatenate([*cross_parts(sums[0:3], at_b[0:3]), pad], axis=0)
        near_vel[b] = (near - jnp.concatenate([sums[4:7], pad], axis=0)) * inv_four_pi

    first = 3 * z.boxes // 8
    loop(1, n_box, lambda d: along_box(d).start())
    loop(0, first, near_box, 4)
    loop(1, n_box, lambda d: along_box(d).wait())
    loop(1, n_age, lambda d: along_age(d).start())
    loop(first, z.boxes, near_box, 4)
    loop(1, n_age, lambda d: along_age(d).wait())
    load_translation.wait()

    every = dot(counts[...], blocks[...].reshape(z.box_total, z.coef))
    for h in range(z.coef // LANES):
        mixed[h] = every[:, h * LANES : (h + 1) * LANES]
    expansion = jnp.zeros((z.boxes, z.coef), f32)
    for t in range(z.kinds):
        rows = [mixed[h, pl.ds(t, z.boxes, stride=z.kinds), :] for h in range(z.coef // LANES)]
        expansion = expansion + dot(jnp.concatenate(rows, axis=1).astype(bf16), trans[t], NT)
    sums_f[...] = expansion

    def far_box(b):
        row = sums_f[pl.ds(b, 1), :] * COS_TOP
        table = two(
            jnp.concatenate([direction[...] * row, jnp.zeros((5, z.coef), f32)], axis=0)
        )
        far = dot(table, wave_hi[b]) + dot(table, wave_lo[b])
        total = near_vel[b] + far[0:8] + far[8:16]
        vel[b] = total[0:4]

    loop(0, z.boxes, far_box, 16)

    def back_copy(d):
        return pltpu.make_async_remote_copy(
            src_ref=back.at[behind(d)],
            dst_ref=returned.at[me],
            send_sem=back_sem.at[0, d - 1],
            recv_sem=back_sem.at[1, d - 1],
            device_id=place(behind(d)),
            device_id_type=MESH,
        )

    def spread(ref, rows):
        high, low = pieces(ref[...].reshape(rows, ref.shape[2]), 2)
        return high.astype(bf16), low.astype(bf16)

    def pick(made, row, kinds, start):
        half = sublane(8, row.shape[1]) // 4
        even = jnp.where(half == 0, row, row - 1.0)
        total = made[0:8]
        for k in range(2, kinds, 2):
            total = jnp.where(even == float(k + start), made[4 * k : 4 * k + 8], total)
        total = jnp.where(lax.rem((row - start).astype(i32), 2) == half, total, 0.0)
        total = jnp.where(row >= float(start), total, 0.0)
        return total[0:4] + total[4:8]

    per_chunk = z.per_chunk

    def send_back(t):
        high, low = spread(vel, 4 * z.boxes)
        for u in range(z.batch):
            c = t * z.batch + u
            hot_u = hot_dst[t, :, u * WIDE : (u + 1) * WIDE]
            made = dot(high, hot_u) + dot(low, hot_u)
            done = pick(made, label_dst[c], z.boxes, 1)
            for v in range(per_chunk):
                d = c * per_chunk + v
                back[behind(d)] = done[:, v * z.per_peer : (v + 1) * z.per_peer]
        start = t * z.batch * per_chunk
        loop(
            jnp.maximum(start, 1), start + z.batch * per_chunk, lambda d: back_copy(d).start()
        )

    loop(0, z.chunks // z.batch, send_back)
    returned[me] = back[me]
    loop(1, groups, lambda d: back_copy(d).wait())

    high, low = spread(returned, 4 * groups)
    for s in range(z.nodes // 512):
        here = slice(s * 512, (s + 1) * 512)
        made = dot(high, hot_src[:, here]) + dot(low, hot_src[:, here])
        out[:, here] = pick(made, owner_row[:, here], groups, 0)[0:3]


def per_device(
    n_age,
    n_box,
    position,
    strength,
    node_box,
    box_order,
    box_center,
    near_list,
    m2l_source,
    m2l_type,
    basis_dir,
    basis_freq,
    basis_phase,
    translation,
):
    z = Sizes(
        n_age, n_box, position.shape[1], box_order.shape[0], basis_phase.shape[0],
        translation.shape[0], m2l_source.shape[1], near_list.shape[1],
    )
    vm = pl.BlockSpec(memory_space=pltpu.VMEM)
    sm = pl.BlockSpec(memory_space=pltpu.SMEM)
    dma = pltpu.SemaphoreType.DMA

    def buf(shape, dtype=f32):
        return pltpu.VMEM(shape, dtype)

    return pl.pallas_call(
        functools.partial(body, z),
        out_shape=jax.ShapeDtypeStruct((3, z.nodes), f32),
        in_specs=[vm, vm, vm, vm, sm, vm, vm, vm, vm, vm, vm, pl.BlockSpec(memory_space=pl.ANY)],
        out_specs=vm,
        scratch_shapes=[
            buf((1, LANES), i32),
            buf((z.groups, 1, LANES), i32),
            buf((8, z.box_total), i32),
            buf((z.groups, 8, z.per_peer)),
            buf((z.groups, 8, z.per_peer)),
            buf((n_age, n_box, z.boxes, z.coef), bf16),
            buf((z.groups, 4, z.per_peer)),
            buf((z.groups, 4, z.per_peer)),
            buf((8, LANES), i32),
            pltpu.SMEM((8, LANES), i32),
            buf(translation.shape, bf16),
            buf((16, z.nodes), bf16),
            buf((z.per_peer, z.nodes), bf16),
            buf((1, z.nodes)),
            buf((16 * z.boxes, z.batch * WIDE), bf16),
            buf((z.chunks // z.batch, z.per_box, z.batch * WIDE), bf16),
            buf((z.chunks, 1, WIDE)),
            buf((16 * z.boxes, z.per_box)),
            buf((z.boxes, 8, z.per_box)),
            buf((z.boxes + 1, 16, z.per_box), bf16),
            buf((z.boxes + 1, z.per_box, 32), bf16),
            buf((z.boxes, 32, z.per_box), bf16),
            buf((z.coef, 48), bf16),
            buf((z.boxes, z.coef, z.per_box), bf16),
            buf((z.boxes, z.coef, z.per_box), bf16),
            buf((z.boxes, z.coef)),
            buf((z.kinds * z.boxes, z.box_total), bf16),
            buf((z.coef // LANES, z.kinds * z.boxes, LANES)),
            buf((z.boxes, 8, z.per_box)),
            buf((z.boxes, 4, z.per_box)),
            dma((2,)),
            dma((2, z.groups - 1)),
            dma((2, z.groups - 1)),
            dma((2, n_age + n_box - 2)),
            dma((2, z.groups - 1)),
        ],
        compiler_params=pltpu.CompilerParams(
            collective_id=0, has_side_effects=True, vmem_limit_bytes=VMEM_LIMIT
        ),
    )(
        position,
        strength,
        node_box.reshape(1, -1),
        box_order.reshape(1, -1),
        box_center,
        near_list.T,
        m2l_source,
        m2l_type,
        basis_dir,
        basis_freq,
        basis_phase.reshape(1, -1),
        translation,
    )


def solution(mesh):
    n_box = mesh.shape["box"]
    n_age = mesh.shape["age"]
    placed = (
        P(None, AXES),
        P(None, AXES),
        P(AXES),
        P(AXES),
        P(None, AXES),
        P(AXES, None),
        P(AXES, None),
        P(AXES, None),
        P(),
        P(),
        P(),
        P(),
    )
    return jax.shard_map(
        functools.partial(per_device, n_age, n_box),
        mesh=mesh,
        in_specs=placed,
        out_specs=P(None, AXES),
        check_vma=False,
    )
```
